512 devices in a mesh: dp: 32 (over y, x), seq: 16 (over z, core).
Axes of the slice: x: 4, y: 8, z: 8, core: 2. Of those that a mesh axis runs over, the one named last changes fastest.
Arguments:
- queries: bfloat16 [32, 2048, 512], P('dp', 'seq'), may hold values from -6 to 6
- keys: bfloat16 [32, 2048, 512], P('dp', 'seq'), may hold values from -6 to 6
- values: bfloat16 [32, 2048, 512], P('dp', 'seq'), may hold values from -6 to 6
- grad_out: bfloat16 [32, 2048, 512], P('dp', 'seq'), may hold values from -6 to 6
- random_blocks: int32 [32, 32, 3], P('dp', 'seq'), may hold values from 0 to 31, as said below
- proj: bfloat16 [512, 512], P('dp'), may hold values from -0.25 to 0.25
Outputs:
- grad_queries: bfloat16 [32, 2048, 512], P('dp', 'seq')
- grad_keys: bfloat16 [32, 2048, 512], P('dp', 'seq')
- grad_values: bfloat16 [32, 2048, 512], P('dp', 'seq')
- grad_proj: float32 [512, 512], P('dp')
The draws below stay inside these ranges and needn't reach their ends.
Inputs may be any that keep to these rules, and one draw needn't show every extreme that they name: `random_blocks`: A query block's random blocks lie outside the 2 blocks of its own index of seq; of the 6 random blocks of one index of seq, at most 1 lie on the blocks of any one other index, and exactly 1 on some.
All inputs are finite; a program needn't handle non-finite values.
Results may differ from the reference program's by a relative error of at most 0.029.
Values may be sent and summed in bfloat16 or wider, within the bound.
A program may use at most 64 MiB of HBM per device.

```python
import jax
import jax.numpy as jnp
from jax import lax

HEADS = 8
HEAD_DIM = 64
BLOCK = 64
RANDOM = 3
QBLOCKS = 2
WIDTH = 512
TOK_DEV = 128
BLOCKS = 32
SEQ_LEN = 2048
BATCH = 32
N_SEQ = 16


def draw_queries(key, part):
    key = jax.random.fold_in(key, 1)
    drawn = jnp.clip(jax.random.normal(key, (BATCH, SEQ_LEN, WIDTH), jnp.float32), -6.0, 6.0)
    return drawn.astype(jnp.bfloat16)


def draw_keys(key, part):
    key = jax.random.fold_in(key, 3)
    drawn = jnp.clip(jax.random.normal(key, (BATCH, SEQ_LEN, WIDTH), jnp.float32), -6.0, 6.0)
    return drawn.astype(jnp.bfloat16)


def draw_random_blocks(key, part):
    key = jax.random.fold_in(key, 5)
    capacity = (QBLOCKS * RANDOM + N_SEQ - 2) // (N_SEQ - 1)
    requests = QBLOCKS * RANDOM

    def one_device(subkey, device):
        ranks = jnp.arange((N_SEQ - 1) * capacity, dtype=jnp.int32) // capacity
        order = jax.random.permutation(subkey, (N_SEQ - 1) * capacity)
        picked = ranks[order][:requests]
        owner = picked + (picked >= device).astype(jnp.int32)
        within = jax.random.randint(jax.random.fold_in(subkey, 1), (requests,), 0, QBLOCKS)
        return (owner * QBLOCKS + within).reshape(QBLOCKS, RANDOM)
    subkeys = jax.random.split(key, BATCH * N_SEQ)
    devices = jnp.tile(jnp.arange(N_SEQ, dtype=jnp.int32), BATCH)
    drawn = jax.vmap(one_device)(subkeys, devices)
    return drawn.reshape(BATCH, BLOCKS, RANDOM).astype(jnp.int32)


def level_of(key, extent, cuts, least, largest):
    def one(dim, blocks):
        draws = jax.random.uniform(jax.random.fold_in(jax.random.fold_in(key, 6), dim), (blocks,), jnp.float32, least / len(cuts), largest / len(cuts))
        return jnp.repeat(jnp.exp(draws), extent[dim] // blocks).reshape((-1,) + (1,) * (len(extent) - dim - 1))

    gain = one(*cuts[0])
    for cut in cuts[1:]:
        gain = gain * one(*cut)
    return gain


def noise(rng, shape, deviation, limit, cuts=(), held_as=jnp.bfloat16):
    loudness = level_of(rng, shape, cuts, -0.22, 0.18) if cuts else 1.0
    entries = jax.random.normal(rng, shape, jnp.float32) * deviation * loudness
    return jnp.minimum(jnp.maximum(entries, -limit), limit).astype(held_as)


def setup_inputs(seed: int = 0) -> dict:
    splits = jax.random.split(jax.random.key(seed), 7)
    return {
        "queries": draw_queries(jax.random.fold_in(splits[6], 71), 0),
        "keys": draw_keys(jax.random.fold_in(splits[6], 71), 0),
        "values": noise(splits[2], (BATCH, SEQ_LEN, WIDTH), 1.0, 6.0, ((0, 32), (1, 16))),
        "grad_out": noise(splits[3], (BATCH, SEQ_LEN, WIDTH), 1.0, 6.0, ((0, 32), (1, 16))),
        "random_blocks": draw_random_blocks(jax.random.fold_in(splits[6], 71), 0),
        "proj": noise(splits[5], (WIDTH, WIDTH), WIDTH ** -0.5, 0.25, ((0, 32),)),
    }


def slot_table(rows, random_ids, total):
    rows = rows.astype(jnp.int32)[:, None]
    fixed = jnp.concatenate([rows - 1, rows, rows + 1, jnp.zeros_like(rows), jnp.ones_like(rows)], axis=1)
    block_ids = jnp.concatenate([fixed, random_ids.astype(jnp.int32)], axis=1)
    width_slots = block_ids.shape[1]
    inside = (block_ids >= 0) & (block_ids < total)
    order = jnp.arange(width_slots, dtype=jnp.int32)
    before = order[None, :] < order[:, None]
    clash = (block_ids[:, :, None] == block_ids[:, None, :]) & inside[:, None, :] & before[None, :, :]
    valid = inside & jnp.logical_not(jnp.any(clash, axis=2))
    return block_ids, valid


def lowered(values):
    return lax.optimization_barrier(values.astype(jnp.bfloat16)).astype(jnp.float32)


def sequence_grads(query, keys, values, grad_out, random_ids, proj):
    total = BLOCKS
    count = 5 + RANDOM
    scale = HEAD_DIM ** -0.5
    block_ids, valid = slot_table(jnp.arange(total, dtype=jnp.int32), random_ids, total)
    safe = jnp.clip(block_ids, 0, total - 1)
    grad_attn = jnp.dot(grad_out, proj.T, preferred_element_type=jnp.float32).astype(jnp.bfloat16)
    key_blocks = keys.reshape(total, BLOCK, WIDTH)
    value_blocks = values.reshape(total, BLOCK, WIDTH)
    query_blocks = query.reshape(total, BLOCK, WIDTH)
    grad_blocks = grad_attn.reshape(total, BLOCK, WIDTH)

    def one_block(index):
        pick = safe[index]
        live = valid[index]
        mask = jnp.repeat(live, BLOCK)
        query_heads = query_blocks[index].astype(jnp.float32).reshape(BLOCK, HEADS, HEAD_DIM)
        key_heads = key_blocks[pick].astype(jnp.float32).reshape(count * BLOCK, HEADS, HEAD_DIM)
        value_heads = value_blocks[pick].astype(jnp.float32).reshape(count * BLOCK, HEADS, HEAD_DIM)
        grad_heads = grad_blocks[index].astype(jnp.float32).reshape(BLOCK, HEADS, HEAD_DIM)
        scores = jnp.einsum('ahd,khd->hak', query_heads, key_heads) * scale
        scores = jnp.where(mask[None, None, :], scores, -jnp.inf)
        top = jnp.max(scores, axis=2, keepdims=True)
        lse = top + jnp.log(jnp.sum(jnp.exp(scores - top), axis=2, keepdims=True))
        prob = jnp.exp(scores - lse)
        prob_low = lowered(prob)
        attn = jnp.einsum('hak,khd->ahd', prob_low, value_heads).astype(jnp.bfloat16)
        delta = jnp.sum(grad_heads * attn.astype(jnp.float32), axis=2)
        dprob = jnp.einsum('ahd,khd->hak', grad_heads, value_heads)
        dscore = lowered(scale * prob * (dprob - jnp.transpose(delta)[:, :, None]))
        grad_q = jnp.einsum('hak,khd->ahd', dscore, key_heads).reshape(BLOCK, WIDTH).astype(jnp.bfloat16)
        key_terms = jnp.einsum('hak,ahd->khd', dscore, query_heads).reshape(count, BLOCK, WIDTH)
        value_terms = jnp.einsum('hak,ahd->khd', prob_low, grad_heads).reshape(count, BLOCK, WIDTH)
        diagonal = (jnp.arange(count) == 1)[:, None, None]
        livef = live.astype(jnp.float32)[:, None, None]
        key_terms = jnp.where(diagonal, key_terms, lowered(key_terms * livef))
        value_terms = jnp.where(diagonal, value_terms, lowered(value_terms * livef))
        return attn.reshape(BLOCK, WIDTH), grad_q, key_terms, value_terms

    attn, grad_q, key_terms, value_terms = lax.map(one_block, jnp.arange(total, dtype=jnp.int32))
    targets = jnp.where(valid, block_ids, total).reshape(-1)
    grad_k = jax.ops.segment_sum(key_terms.reshape(total * count, BLOCK * WIDTH), targets, num_segments=total)
    grad_v = jax.ops.segment_sum(value_terms.reshape(total * count, BLOCK * WIDTH), targets, num_segments=total)
    attn_groups = attn.reshape(N_SEQ, TOK_DEV, WIDTH).astype(jnp.float32)
    grad_groups = grad_out.reshape(N_SEQ, TOK_DEV, WIDTH).astype(jnp.float32)
    partial_proj = lowered(jnp.einsum('sta,stb->sab', attn_groups, grad_groups))
    grad_w = jnp.sum(partial_proj, axis=0)
    return (grad_q.reshape(SEQ_LEN, WIDTH), grad_k.reshape(SEQ_LEN, WIDTH).astype(jnp.bfloat16),
            grad_v.reshape(SEQ_LEN, WIDTH).astype(jnp.bfloat16), grad_w)


def reference(queries, keys, values, grad_out, random_blocks, proj):
    def step(carry, items):
        grad_q, grad_k, grad_v, grad_w = sequence_grads(items[0], items[1], items[2], items[3], items[4], proj)
        return carry + grad_w, (grad_q, grad_k, grad_v)

    start = jnp.zeros((WIDTH, WIDTH), jnp.float32)
    grad_proj, (grad_queries, grad_keys, grad_values) = lax.scan(step, start, (queries, keys, values, grad_out, random_blocks))
    return grad_queries, grad_keys, grad_values, grad_proj
```

```python
import functools

import jax
import jax.numpy as jnp
from jax import lax
from jax.experimental import pallas as pl
from jax.experimental.pallas import tpu as pltpu
from jax.sharding import PartitionSpec as P

HEADS = 8
HEAD_DIM = 64
BLOCK = 64
RANDOM = 3
CHIPS = 8
TOKENS = 128
WIDTH = 512
HALF = 256
BLOCKS = 32
SCALE = HEAD_DIM ** (-0.5)
NEG = -1e30
NEAR = (1, 7, 2, 6, 3, 5, 4)
FAR = (4, 3, 5, 2, 6, 1, 7)

TBL, KV, KVF, QS, GS, PX, PY, PS = 0, 8, 16, 24, 32, 40, 44, 52
DQ, XK, DK, RS, RX, RY, RZ, RF = 56, 64, 72, 80, 84, 88, 96, 104
SEMS = 112


def dot(a, b, dims):
    return lax.dot_general(a, b, (dims, ((), ())), preferred_element_type=jnp.float32)


def kernel(nx, ny, q_ref, k_ref, v_ref, go_ref, rb_ref, pj_ref, gq_ref, gk_ref, gv_ref, gp_ref,
           tblme, tblv, tbls, kvp, kv, qp, qr, gpk, gr, pj, acc, trand, dqs, dqr, xs, xr, dks, dkr,
           pp, pps, s1, rx, s2, ry, s3, rz, s4, s4b, ssem, rsem, lsem):
    dp = lax.axis_index("dp")
    s = lax.axis_index("seq")
    z, c = s // 2, s % 2
    y, x = dp // nx, dp % nx
    other = 1 - c
    sib = (dp, 2 * z + other)
    rows = nx * ny * 16

    def zdev(zt):
        return (dp, 2 * zt + c)

    def send(src, dst, sem, dev):
        copy = pltpu.make_async_remote_copy(
            src_ref=src, dst_ref=dst, send_sem=ssem.at[sem], recv_sem=rsem.at[sem],
            device_id=dev, device_id_type=pl.DeviceIdType.MESH)
        copy.start()

    def got(dst, sem):
        pltpu.make_async_remote_copy(
            src_ref=dst, dst_ref=dst, send_sem=ssem.at[sem], recv_sem=rsem.at[sem],
            device_id=sib, device_id_type=pl.DeviceIdType.MESH).wait_recv()

    def sent(src, sem):
        pltpu.make_async_remote_copy(
            src_ref=src, dst_ref=src, send_sem=ssem.at[sem], recv_sem=rsem.at[sem],
            device_id=sib, device_id_type=pl.DeviceIdType.MESH).wait_send()

    def ahead(off):
        return (z + off) % CHIPS

    def behind(off):
        return (z + CHIPS - off) % CHIPS

    barrier = pltpu.get_barrier_semaphore()
    partners = [sib] + [zdev(ahead(off)) for off in range(1, CHIPS)]
    partners += [(y * nx + (x + d) % nx, s) for d in range(1, nx)]
    partners += [(((y + d) % ny) * nx + x, s) for d in range(1, ny)]
    for dev in partners:
        pl.semaphore_signal(barrier, inc=1, device_id=dev, device_id_type=pl.DeviceIdType.MESH)
    pl.semaphore_wait(barrier, len(partners))

    mine = pl.ds(pl.multiple_of(c * HALF, HALF), HALF)
    theirs = pl.ds(pl.multiple_of(other * HALF, HALF), HALF)

    with jax.named_scope("proj_rows_x"):
        own_rows = pl.ds(pl.multiple_of(dp * 16, 16), 16)
        for d in range(1, nx):
            send(pj_ref.at[:, mine], pj.at[c, own_rows], PX + d, (y * nx + (x + d) % nx, s))
        pj[c, own_rows] = pj_ref[:, mine]

    with jax.named_scope("key_value_blocks"):
        lane = lax.broadcasted_iota(jnp.int32, (8, 128), 1)
        row = jnp.zeros((8, 128), jnp.int32)
        for e in range(2 * RANDOM):
            block = rb_ref[0, e // RANDOM, e % RANDOM]
            own = block // 2
            row = jnp.where(lane == own, e, row)
            row = jnp.where(lane == own + 16 + 16 * (block % 2), 1, row)
            row = jnp.where(lane == 48 + e, block, row)
        tblme[...] = row
        tblv[z] = row
        for off in NEAR:
            send(tblme, tblv.at[z], TBL + off, zdev(ahead(off)))
        for h in range(HEADS):
            f = slice(h * HEAD_DIM, (h + 1) * HEAD_DIM)
            packed = jnp.concatenate([k_ref[0, :, f], v_ref[0, :, f]], axis=1)
            kvp[h] = packed.reshape(2, BLOCK, 128)
        kv[pl.ds(2 * s, 2)] = kvp[z]
        for off in FAR:
            zt = ahead(off)
            send(kvp.at[zt], kv.at[pl.ds(2 * s, 2)], KV + off, zdev(zt))
        send(kvp.at[z], kv.at[pl.ds(2 * s, 2)], KVF, sib)

    with jax.named_scope("query_blocks"):
        for h in range(HEADS):
            f = slice(h * HEAD_DIM, (h + 1) * HEAD_DIM)
            qp[h] = jnp.concatenate([q_ref[0, :BLOCK, f], q_ref[0, BLOCK:, f]], axis=1)
        qr[z] = qp[z]
        for off in FAR:
            zt = ahead(off)
            send(qp.at[zt], qr.at[z], QS + off, zdev(zt))

    with jax.named_scope("proj_rows_y"):
        group = nx * 16
        own_group = pl.ds(pl.multiple_of(y * group, group), group)
        for d in range(1, nx):
            xf = (x + nx - d) % nx
            got(pj.at[c, pl.ds(pl.multiple_of((y * nx + xf) * 16, 16), 16)], PX + d)
        for d in range(1, ny):
            send(pj.at[c, own_group], pj.at[c, own_group], PY + d, (((y + d) % ny) * nx + x, s))

    acc[...] = jnp.zeros_like(acc)

    with jax.named_scope("proj_rows_y_wait"):
        for d in range(1, ny):
            yf = (y + ny - d) % ny
            got(pj.at[c, pl.ds(pl.multiple_of(yf * group, group), group)], PY + d)
        send(pj.at[c], pj.at[c], PS, sib)

    def forward(off):
        zf = behind(off)
        part = kv.at[pl.ds(4 * zf + 2 * c, 2)]
        got(part, KV + off)
        send(part, part, KVF + off, sib)

    for off in NEAR[:4]:
        forward(off)

    with jax.named_scope("grad_attn"):
        got(pj.at[other], PS)
        ga = dot(go_ref[0, :, :HALF], pj[0], ((1,), (1,)))
        ga += dot(go_ref[0, :, HALF:], pj[1], ((1,), (1,)))
        ga = ga.astype(jnp.bfloat16)
        for h in range(HEADS):
            f = slice(h * HEAD_DIM, (h + 1) * HEAD_DIM)
            gpk[h] = jnp.concatenate([ga[:BLOCK, f], ga[BLOCK:, f]], axis=1)
        gr[z] = gpk[z]
        for off in FAR:
            zt = ahead(off)
            send(gpk.at[zt], gr.at[z], GS + off, zdev(zt))

    for off in NEAR[4:]:
        forward(off)
    for off in NEAR:
        got(tblv.at[behind(off)], TBL + off)
    table = pltpu.make_async_copy(tblv, tbls, lsem.at[0])
    table.start()
    table.wait()
    for off in (0,) + NEAR:
        got(kv.at[pl.ds(4 * behind(off) + 2 * other, 2)], KVF + off)

    slot = lax.broadcasted_iota(jnp.int32, (1, 8 * BLOCK), 1) // BLOCK
    low = lax.broadcasted_iota(jnp.int32, (BLOCK, 128), 1) < HEAD_DIM

    def attend(zs, b, qf, gf):
        i = 4 * zs + 2 * c + b
        before, after = jnp.maximum(i - 1, 0), jnp.minimum(i + 1, BLOCKS - 1)
        ids = [tbls[zs, 0, 48 + RANDOM * b + n] for n in range(RANDOM)]
        valid = [i >= 1, i >= 0, i < BLOCKS - 1, i >= 2, i >= 3]
        for n in range(RANDOM):
            r = ids[n]
            clash = (r == i - 1) | (r == i) | (r == i + 1) | (r <= 1)
            for earlier in ids[:n]:
                clash = clash | (r == earlier)
            valid.append(jnp.logical_not(clash))
        bias = jnp.zeros((1, 8 * BLOCK), jnp.float32)
        for n in range(8):
            bias = jnp.where(slot == n, jnp.where(valid[n], 0.0, NEG), bias)
        tiles = jnp.concatenate(
            [kv[before], kv[i], kv[after], kv[0], kv[1]] + [kv[r] for r in ids], axis=0)
        if b == 0:
            gf = jnp.concatenate([gf[:, HEAD_DIM:], gf[:, :HEAD_DIM]], axis=1)
        else:
            qf = jnp.concatenate([qf[:, HEAD_DIM:], qf[:, :HEAD_DIM]], axis=1)
        zero = jnp.zeros_like(qf)
        ql = jnp.where(low, qf, zero)
        gl = jnp.where(low, zero, gf)
        both = dot(jnp.concatenate([ql, gl], axis=0), tiles, ((1,), (1,)))
        scores = both[:BLOCK] * SCALE + bias
        dprob = both[BLOCK:]
        top = jnp.max(scores, axis=1, keepdims=True)
        e = jnp.exp(scores - top)
        prob = e * (1.0 / jnp.sum(e, axis=1, keepdims=True))
        delta = jnp.sum(prob * dprob, axis=1, keepdims=True)
        dscore = prob * (dprob - delta) * SCALE
        pd = jnp.concatenate([prob, dscore], axis=0).astype(jnp.bfloat16)
        out = dot(pd, tiles, ((1,), (0,)))
        terms = dot(pd, jnp.concatenate([gl, ql], axis=0), ((0,), (0,)))
        for n, j in enumerate((before, i, after, 0, 1)):
            acc[j] += terms[n * BLOCK:(n + 1) * BLOCK]
        for n in range(RANDOM):
            trand[zs * 2 * RANDOM + RANDOM * b + n] = terms[(5 + n) * BLOCK:(6 + n) * BLOCK]
        dqs[zs, b] = jnp.where(low, out[BLOCK:], out[:BLOCK]).astype(jnp.bfloat16)

    def offset(step):
        odd = step % 2
        return (odd * ((step + 1) // 2) + (1 - odd) * (CHIPS - step // 2)) % CHIPS

    with jax.named_scope("attention"):
        @pl.loop(0, CHIPS)
        def _(step):
            off = offset(step)
            zs = behind(off)

            @pl.when(step > 0)
            def _():
                got(qr.at[zs], QS + off)
                got(gr.at[zs], GS + off)

            qf, gf = qr[zs], gr[zs]
            for b in range(2):
                attend(zs, b, qf, gf)

            @pl.when(step > 0)
            def _():
                send(dqs.at[zs], dqr.at[z], DQ + off, zdev(zs))

        dqr[z] = dqs[z]

    def pull(o):
        parts = [acc[2 * o], acc[2 * o + 1]]
        for zs in range(CHIPS):
            term = trand[zs * 2 * RANDOM + tbls[zs, 0, o]]
            for w in range(2):
                parts[w] += term * tbls[zs, 0, 16 + 16 * w + o].astype(jnp.float32)
        return parts

    with jax.named_scope("other_core_terms"):
        @pl.loop(0, CHIPS)
        def _(k):
            parts = pull(2 * k + other)
            for w in range(2):
                xs[k, w] = parts[w].astype(jnp.bfloat16)
            send(xs.at[k], xr.at[k], XK + k, sib)

    with jax.named_scope("partial_proj"):
        for off in NEAR:
            got(dqr.at[ahead(off)], DQ + off)
        pieces = [dqr[h].reshape(TOKENS, 128) for h in range(HEADS)]
        attn = jnp.concatenate([p[:, HEAD_DIM:] for p in pieces], axis=1)
        for half in range(2):
            f = slice(half * HALF, (half + 1) * HALF)
            pp[half] = dot(attn, go_ref[0, :, f], ((0,), (0,))).astype(jnp.bfloat16)
        send(pp.at[other], pps, RS, sib)
        gq_ref[0] = jnp.concatenate([p[:, :HEAD_DIM] for p in pieces], axis=1)

    with jax.named_scope("own_terms"):
        @pl.loop(0, CHIPS)
        def _(step):
            off = (step + 4) % CHIPS
            k = ahead(off)
            parts = pull(2 * k + c)
            got(xr.at[k], XK + k)
            for w in range(2):
                dks[k, w] = (parts[w] + xr[k, w].astype(jnp.float32)).astype(jnp.bfloat16)

            @pl.when(off > 0)
            def _():
                send(dks.at[k], dkr.at[z], DK + off, zdev(k))

        dkr[z] = dks[z]

    def wide(ref):
        return ref.astype(jnp.float32)

    with jax.named_scope("grad_proj_x"):
        got(pps, RS)
        s1[...] = (wide(pp[c]) + wide(pps[...])).astype(jnp.bfloat16).reshape(ny, nx, 16, HALF)
        for d in range(1, nx):
            xt = (x + d) % nx
            send(s1.at[:, xt], rx.at[d], RX + d, (y * nx + xt, s))
        total = wide(s1[:, x])
        for d in range(1, nx):
            got(rx.at[d], RX + d)
            total += wide(rx[d])
        s2[...] = total.astype(jnp.bfloat16)
    with jax.named_scope("grad_proj_y"):
        for d in range(1, ny):
            yt = (y + d) % ny
            send(s2.at[yt], ry.at[d], RY + d, (yt * nx + x, s))
        total = wide(s2[y])
        for d in range(1, ny):
            got(ry.at[d], RY + d)
            total += wide(ry[d])
        s3[...] = total.astype(jnp.bfloat16)
    with jax.named_scope("grad_proj_z"):
        rz[z] = s3[...]
        for off in FAR:
            send(s3, rz.at[z], RZ + off, zdev(ahead(off)))
        for off in NEAR:
            got(rz.at[behind(off)], RZ + off)
        total = wide(rz[0])
        for k in range(1, CHIPS):
            total += wide(rz[k])
        s4[...] = total
        send(s4, s4b, RF, sib)
        gp_ref[:, mine] = total

    with jax.named_scope("grad_keys_values"):
        for off in NEAR:
            got(dkr.at[behind(off)], DK + off)
        pieces = [dkr[h].reshape(TOKENS, 128) for h in range(HEADS)]
        gk_ref[0] = jnp.concatenate([p[:, :HEAD_DIM] for p in pieces], axis=1)
        gv_ref[0] = jnp.concatenate([p[:, HEAD_DIM:] for p in pieces], axis=1)

    got(s4b, RF)
    gp_ref[:, theirs] = s4b[...]

    with jax.named_scope("sent"):
        for d in range(1, nx):
            sent(pj_ref.at[:, mine], PX + d)
            sent(s1.at[:, (x + d) % nx], RX + d)
        for d in range(1, ny):
            sent(pj.at[c, own_group], PY + d)
            sent(s2.at[(y + d) % ny], RY + d)
        sent(pj.at[c], PS)
        sent(pp.at[other], RS)
        sent(s4, RF)
        sent(kvp.at[z], KVF)
        sent(xs.at[0], XK)
        for off in range(1, CHIPS):
            zt, zf = ahead(off), behind(off)
            sent(tblme, TBL + off)
            sent(kvp.at[zt], KV + off)
            sent(kv.at[pl.ds(4 * zf + 2 * c, 2)], KVF + off)
            sent(qp.at[zt], QS + off)
            sent(gpk.at[zt], GS + off)
            sent(dqs.at[zf], DQ + off)
            sent(xs.at[off], XK + off)
            sent(dks.at[zt], DK + off)
            sent(s3, RZ + off)


def attention_grads(nx, ny, q, k, v, go, rb, proj):
    bf, f32 = jnp.bfloat16, jnp.float32
    rows = nx * ny * 16
    vmem = pl.BlockSpec(memory_space=pltpu.VMEM)
    smem = pl.BlockSpec(memory_space=pltpu.SMEM)
    scratch = [
        pltpu.VMEM((8, 128), jnp.int32),
        pltpu.VMEM((CHIPS, 8, 128), jnp.int32),
        pltpu.SMEM((CHIPS, 8, 128), jnp.int32),
        pltpu.VMEM((HEADS, 2, BLOCK, 128), bf),
        pltpu.VMEM((BLOCKS, BLOCK, 128), bf),
        pltpu.VMEM((HEADS, BLOCK, 128), bf),
        pltpu.VMEM((CHIPS, BLOCK, 128), bf),
        pltpu.VMEM((HEADS, BLOCK, 128), bf),
        pltpu.VMEM((CHIPS, BLOCK, 128), bf),
        pltpu.VMEM((2, rows, HALF), bf),
        pltpu.VMEM((BLOCKS, BLOCK, 128), f32),
        pltpu.VMEM((CHIPS * 2 * RANDOM, BLOCK, 128), f32),
        pltpu.VMEM((CHIPS, 2, BLOCK, 128), bf),
        pltpu.VMEM((HEADS, 2, BLOCK, 128), bf),
        pltpu.VMEM((CHIPS, 2, BLOCK, 128), bf),
        pltpu.VMEM((CHIPS, 2, BLOCK, 128), bf),
        pltpu.VMEM((CHIPS, 2, BLOCK, 128), bf),
        pltpu.VMEM((HEADS, 2, BLOCK, 128), bf),
        pltpu.VMEM((2, rows, HALF), bf),
        pltpu.VMEM((rows, HALF), bf),
        pltpu.VMEM((ny, nx, 16, HALF), bf),
        pltpu.VMEM((nx, ny, 16, HALF), bf),
        pltpu.VMEM((ny, 16, HALF), bf),
        pltpu.VMEM((ny, 16, HALF), bf),
        pltpu.VMEM((16, HALF), bf),
        pltpu.VMEM((CHIPS, 16, HALF), bf),
        pltpu.VMEM((16, HALF), f32),
        pltpu.VMEM((16, HALF), f32),
        pltpu.SemaphoreType.DMA((SEMS,)),
        pltpu.SemaphoreType.DMA((SEMS,)),
        pltpu.SemaphoreType.DMA((1,)),
    ]
    tokens = jax.ShapeDtypeStruct((1, TOKENS, WIDTH), bf)
    return pl.pallas_call(
        functools.partial(kernel, nx, ny),
        out_shape=[tokens, tokens, tokens, jax.ShapeDtypeStruct((16, WIDTH), f32)],
        in_specs=[vmem, vmem, vmem, vmem, smem, vmem],
        out_specs=[vmem, vmem, vmem, vmem],
        scratch_shapes=scratch,
        compiler_params=pltpu.CompilerParams(
            collective_id=0, has_side_effects=True, vmem_limit_bytes=32 * 1024 * 1024),
        cost_estimate=pl.CostEstimate(
            flops=2 * 500_000_000, bytes_accessed=2_000_000, transcendentals=600_000),
    )(q, k, v, go, rb, proj)


def solution(mesh, nx=4, ny=8):
    tokens = P("dp", "seq", None)
    return jax.shard_map(
        functools.partial(attention_grads, nx, ny),
        mesh=mesh,
        in_specs=(tokens, tokens, tokens, tokens, tokens, P("dp", None)),
        out_specs=(tokens, tokens, tokens, P("dp", None)),
        check_vma=False,
    )
```

```python
import functools

import jax
import jax.numpy as jnp
from jax import lax
from jax.experimental import pallas as pl
from jax.experimental.pallas import tpu as pltpu
from jax.sharding import PartitionSpec as P

HEADS = 8
HEAD_DIM = 64
BLOCK = 64
RANDOM = 3
CHIPS = 8
TOKENS = 128
WIDTH = 512
HALF = 256
BLOCKS = 32
SCALE = HEAD_DIM ** (-0.5)
NEG = -1e30
NEAR = (1, 7, 2, 6, 3, 5, 4)
FAR = (4, 3, 5, 2, 6, 1, 7)

TBL, KV, KVF, QS, GS, PY, PX, PS = 0, 8, 16, 24, 32, 40, 48, 52
AT, DQ, XK, DK, RS, RX, RY, RZ, RF = 56, 64, 72, 80, 88, 92, 96, 104, 112
SEMS = 116


def dot(a, b, dims):
    return lax.dot_general(a, b, (dims, ((), ())), preferred_element_type=jnp.float32)


def halves(a, b):
    return jnp.concatenate([a, b], axis=1)


def kernel(nx, ny, q_hbm, k_hbm, v_hbm, go_hbm, rb_hbm, pj_hbm, gq_ref, gk_ref, gv_ref, gp_ref,
           q_ref, k_ref, v_ref, go_ref, rb_ref, pj_ref,
           tblme, tblv, tbls, kvp, kv, qp, qr, gpk, gr, pj, pst, acc, trand, ats, atr, dqs, dqr,
           xs, xr, dks, dkr, pp, pps, s1, rx, s2, ry, s3, rz, s4, s4b, ssem, rsem, lsem):
    dp = lax.axis_index("dp")
    s = lax.axis_index("seq")
    z, c = s // 2, s % 2
    y, x = dp // nx, dp % nx
    other = 1 - c
    sib = (dp, 2 * z + other)

    def zdev(zt):
        return (dp, 2 * zt + c)

    def xdev(d):
        return (y * nx + (x + d) % nx, s)

    def ydev(d):
        return (((y + d) % ny) * nx + x, s)

    def send(src, dst, sem, dev):
        copy = pltpu.make_async_remote_copy(
            src_ref=src, dst_ref=dst, send_sem=ssem.at[sem], recv_sem=rsem.at[sem],
            device_id=dev, device_id_type=pl.DeviceIdType.MESH)
        copy.start()

    def got(dst, sem):
        pltpu.make_async_remote_copy(
            src_ref=dst, dst_ref=dst, send_sem=ssem.at[sem], recv_sem=rsem.at[sem],
            device_id=sib, device_id_type=pl.DeviceIdType.MESH).wait_recv()

    def sent(src, sem):
        pltpu.make_async_remote_copy(
            src_ref=src, dst_ref=src, send_sem=ssem.at[sem], recv_sem=rsem.at[sem],
            device_id=sib, device_id_type=pl.DeviceIdType.MESH).wait_send()

    def ahead(off):
        return (z + off) % CHIPS

    def behind(off):
        return (z + CHIPS - off) % CHIPS

    barrier = pltpu.get_barrier_semaphore()
    partners = [sib] + [zdev(ahead(off)) for off in range(1, CHIPS)]
    partners += [xdev(d) for d in range(1, nx)] + [ydev(d) for d in range(1, ny)]
    for dev in partners:
        pl.semaphore_signal(barrier, inc=1, device_id=dev, device_id_type=pl.DeviceIdType.MESH)

    loads = [pltpu.make_async_copy(a, b, lsem.at[1 + n]) for n, (a, b) in enumerate((
        (pj_hbm, pj_ref), (rb_hbm, rb_ref), (k_hbm, k_ref), (v_hbm, v_ref), (q_hbm, q_ref),
        (go_hbm, go_ref)))]
    for load in loads:
        load.start()

    mine = pl.ds(pl.multiple_of(c * HALF, HALF), HALF)
    theirs = pl.ds(pl.multiple_of(other * HALF, HALF), HALF)

    with jax.named_scope("pack_inputs"):
        loads[0].wait()
        loads[1].wait()
        pj[c, y, x] = pj_ref[:, mine]
        lane = lax.broadcasted_iota(jnp.int32, (8, 128), 1)
        row = jnp.zeros((8, 128), jnp.int32)
        for e in range(2 * RANDOM):
            block = rb_ref[0, e // RANDOM, e % RANDOM]
            own = block // 2
            row = jnp.where(lane == own, e, row)
            row = jnp.where(lane == own + 16 + 16 * (block % 2), 1, row)
            row = jnp.where(lane == 48 + e, block, row)
        tblme[...] = row
        tblv[z] = row
        loads[2].wait()
        loads[3].wait()
        for h in range(HEADS):
            f = slice(h * HEAD_DIM, (h + 1) * HEAD_DIM)
            kvp[h] = halves(k_ref[0, :, f], v_ref[0, :, f]).reshape(2, BLOCK, 128)
        kv[pl.ds(2 * s, 2)] = kvp[z]
        loads[4].wait()
        for h in range(HEADS):
            f = slice(h * HEAD_DIM, (h + 1) * HEAD_DIM)
            qp[h] = halves(q_ref[0, :BLOCK, f], q_ref[0, BLOCK:, f])
        qr[z] = qp[z]

    with jax.named_scope("barrier"):
        pl.semaphore_wait(barrier, len(partners))

    with jax.named_scope("first_sends"):
        for d in range(1, ny):
            send(pj_ref.at[:, mine], pj.at[c, y, x], PY + d, ydev(d))
        for off in FAR:
            zt = ahead(off)
            send(kvp.at[zt], kv.at[pl.ds(2 * s, 2)], KV + off, zdev(zt))
        send(kvp.at[z], kv.at[pl.ds(2 * s, 2)], KVF, sib)
        for off in FAR:
            send(tblme, tblv.at[z], TBL + off, zdev(ahead(off)))
        for off in FAR:
            zt = ahead(off)
            send(qp.at[zt], qr.at[z], QS + off, zdev(zt))

    acc[...] = jnp.zeros_like(acc)

    with jax.named_scope("proj_rows_y"):
        for d in range(1, ny):
            got(pj.at[c, (y + ny - d) % ny, x], PY + d)
        for d in range(1, nx):
            send(pj.at[c, :, x], pj.at[c, :, x], PX + d, xdev(d))

    def forward(off):
        zf = behind(off)
        part = kv.at[pl.ds(4 * zf + 2 * c, 2)]
        got(part, KV + off)
        send(part, part, KVF + off, sib)

    with jax.named_scope("forward_a"):
        for off in NEAR[:4]:
            forward(off)

    with jax.named_scope("proj_rows_x"):
        for d in range(1, nx):
            got(pj.at[c, :, (x + nx - d) % nx], PX + d)
        send(pj.at[c], pj.at[c], PS, sib)

    with jax.named_scope("forward_b"):
        for off in NEAR[4:]:
            forward(off)

    with jax.named_scope("proj_other"):
        got(pj.at[other], PS)
        loads[5].wait()
    with jax.named_scope("grad_attn"):
        rows = nx * ny * 16
        ga = dot(go_ref[0, :, :HALF], pj[0].reshape(rows, HALF), ((1,), (1,)))
        ga += dot(go_ref[0, :, HALF:], pj[1].reshape(rows, HALF), ((1,), (1,)))
        ga = ga.astype(jnp.bfloat16)
        for h in range(HEADS):
            f = slice(h * HEAD_DIM, (h + 1) * HEAD_DIM)
            gpk[h] = halves(ga[:BLOCK, f], ga[BLOCK:, f])
        gr[z] = gpk[z]
        for off in FAR:
            zt = ahead(off)
            send(gpk.at[zt], gr.at[z], GS + off, zdev(zt))

    with jax.named_scope("tables"):
        for off in NEAR:
            got(tblv.at[behind(off)], TBL + off)
        table = pltpu.make_async_copy(tblv, tbls, lsem.at[0])
        table.start()
        table.wait()
    with jax.named_scope("other_core_keys"):
        for off in (0,) + NEAR:
            got(kv.at[pl.ds(4 * behind(off) + 2 * other, 2)], KVF + off)

    slot = lax.broadcasted_iota(jnp.int32, (1, 8 * BLOCK), 1) // BLOCK
    low = lax.broadcasted_iota(jnp.int32, (BLOCK, 128), 1) < HEAD_DIM

    def swap(a):
        return halves(a[:, HEAD_DIM:], a[:, :HEAD_DIM])

    def slots(zs, b):
        i = 4 * zs + 2 * c + b
        fixed = (jnp.maximum(i - 1, 0), i, jnp.minimum(i + 1, BLOCKS - 1), 0, 1)
        return i, fixed, [tbls[zs, 0, 48 + RANDOM * b + n] for n in range(RANDOM)]

    def tiles_of(fixed, ids):
        return jnp.concatenate([kv[j] for j in fixed] + [kv[r] for r in ids], axis=0)

    def softmax(zs, b, ql):
        i, fixed, ids = slots(zs, b)
        valid = [i >= 1, i >= 0, i < BLOCKS - 1, i >= 2, i >= 3]
        for n in range(RANDOM):
            r = ids[n]
            clash = (r == i - 1) | (r == i) | (r == i + 1) | (r <= 1)
            for earlier in ids[:n]:
                clash = clash | (r == earlier)
            valid.append(jnp.logical_not(clash))
        bias = jnp.zeros((1, 8 * BLOCK), jnp.float32)
        for n in range(8):
            bias = jnp.where(slot == n, jnp.where(valid[n], 0.0, NEG), bias)
        tiles = tiles_of(fixed, ids)
        scores = dot(ql, tiles, ((1,), (1,))) * SCALE + bias
        top = jnp.max(scores, axis=1, keepdims=True)
        e = jnp.exp(scores - top)
        prob = (e * (1.0 / jnp.sum(e, axis=1, keepdims=True))).astype(jnp.bfloat16)
        pst[zs, b] = prob
        return dot(prob, tiles, ((1,), (0,)))

    def backward(zs, b, ql, gl):
        _, fixed, ids = slots(zs, b)
        tiles = tiles_of(fixed, ids)
        dprob = dot(gl, tiles, ((1,), (1,)))
        low_prob = pst[zs, b]
        prob = low_prob.astype(jnp.float32)
        delta = jnp.sum(prob * dprob, axis=1, keepdims=True)
        dscore = (prob * (dprob - delta) * SCALE).astype(jnp.bfloat16)
        both = jnp.concatenate([low_prob, dscore], axis=0)
        terms = dot(both, jnp.concatenate([gl, ql], axis=0), ((0,), (0,)))
        for n, j in enumerate(fixed):
            acc[j] += terms[n * BLOCK:(n + 1) * BLOCK]
        for n in range(RANDOM):
            trand[zs * 2 * RANDOM + RANDOM * b + n] = terms[(5 + n) * BLOCK:(6 + n) * BLOCK]
        return dot(dscore, tiles, ((1,), (0,)))

    def offset(step):
        odd = step % 2
        return (odd * ((step + 1) // 2) + (1 - odd) * (CHIPS - step // 2)) % CHIPS

    def wide(ref):
        return ref.astype(jnp.float32)

    with jax.named_scope("softmax"):
        @pl.loop(0, CHIPS)
        def _(step):
            off = offset(step)
            zs = behind(off)

            @pl.when(step > 0)
            def _():
                got(qr.at[zs], QS + off)

            qf = qr[zs]
            zero = jnp.zeros_like(qf)
            outs = [softmax(zs, b, jnp.where(low, swap(qf) if b else qf, zero)) for b in range(2)]
            ats[zs] = jnp.where(low, swap(outs[0]), outs[1]).astype(jnp.bfloat16)

            @pl.when(step > 0)
            def _():
                send(ats.at[zs], atr.at[z], AT + off, zdev(zs))

        atr[z] = ats[z]

    def partial_proj():
        with jax.named_scope("attn_back"):
            for off in NEAR:
                got(atr.at[ahead(off)], AT + off)
        with jax.named_scope("partial_proj"):
            attn = jnp.concatenate([
                jnp.concatenate([atr[h][:, :HEAD_DIM] for h in range(HEADS)], axis=1),
                jnp.concatenate([atr[h][:, HEAD_DIM:] for h in range(HEADS)], axis=1)], axis=0)
            for half in range(2):
                f = slice(half * HALF, (half + 1) * HALF)
                pp[half] = dot(attn, go_ref[0, :, f], ((0,), (0,))).astype(jnp.bfloat16)
            send(pp.at[other], pps, RS, sib)

    def proj_x():
        with jax.named_scope("grad_proj_x"):
            got(pps, RS)
            total = wide(pp[c]) + wide(pps[...])
            s1[...] = total.astype(jnp.bfloat16).reshape(ny, nx, 16, HALF)
            for d in range(1, nx):
                xt = (x + d) % nx
                send(s1.at[:, xt], rx.at[d], RX + d, xdev(d))

    def proj_y():
        with jax.named_scope("grad_proj_y"):
            total = wide(s1[:, x])
            for d in range(1, nx):
                got(rx.at[d], RX + d)
                total += wide(rx[d])
            s2[...] = total.astype(jnp.bfloat16)
            for d in range(1, ny):
                send(s2.at[(y + d) % ny], ry.at[d], RY + d, ydev(d))

    def proj_z():
        with jax.named_scope("grad_proj_z"):
            total = wide(s2[y])
            for d in range(1, ny):
                got(ry.at[d], RY + d)
                total += wide(ry[d])
            s3[...] = total.astype(jnp.bfloat16)
            rz[z] = s3[...]
            for off in FAR:
                send(s3, rz.at[z], RZ + off, zdev(ahead(off)))

    def proj_core():
        with jax.named_scope("grad_proj_core"):
            for off in NEAR:
                got(rz.at[behind(off)], RZ + off)
            total = wide(rz[0])
            for k in range(1, CHIPS):
                total += wide(rz[k])
            s4[...] = total
            send(s4, s4b, RF, sib)
            gp_ref[:, mine] = total

    with jax.named_scope("gradients"):
        @pl.loop(0, CHIPS)
        def _(step):
            off = offset(step)
            zs = behind(off)

            @pl.when(step > 0)
            def _():
                got(gr.at[zs], GS + off)

            qf, gf = qr[zs], gr[zs]
            zero = jnp.zeros_like(qf)
            outs = [backward(zs, b, jnp.where(low, swap(qf) if b else qf, zero),
                             jnp.where(low, zero, gf if b else swap(gf))) for b in range(2)]
            dqs[zs] = jnp.where(low, outs[0], swap(outs[1])).astype(jnp.bfloat16)

            @pl.when(step > 0)
            def _():
                send(dqs.at[zs], dqr.at[z], DQ + off, zdev(zs))

            pl.when(step == 3)(partial_proj)
            pl.when(step == 5)(proj_x)

        dqr[z] = dqs[z]

    def pull(o):
        parts = [acc[2 * o], acc[2 * o + 1]]
        for zs in range(CHIPS):
            term = trand[zs * 2 * RANDOM + tbls[zs, 0, o]]
            for w in range(2):
                parts[w] += term * tbls[zs, 0, 16 + 16 * w + o].astype(jnp.float32)
        return parts

    with jax.named_scope("other_core_terms"):
        @pl.loop(0, CHIPS)
        def _(step):
            off = (step + 4) % CHIPS
            k = ahead(off)
            parts = pull(2 * k + other)
            for w in range(2):
                xs[k, w] = parts[w].astype(jnp.bfloat16)
            send(xs.at[k], xr.at[k], XK + off, sib)

    proj_y()

    with jax.named_scope("own_terms"):
        @pl.loop(0, CHIPS)
        def _(step):
            off = (step + 4) % CHIPS
            k = ahead(off)
            parts = pull(2 * k + c)
            got(xr.at[k], XK + off)
            for w in range(2):
                dks[k, w] = (parts[w] + xr[k, w].astype(jnp.float32)).astype(jnp.bfloat16)

            @pl.when(off > 0)
            def _():
                send(dks.at[k], dkr.at[z], DK + off, zdev(k))

        dkr[z] = dks[z]

    proj_z()

    with jax.named_scope("grad_queries"):
        for off in NEAR:
            got(dqr.at[ahead(off)], DQ + off)
        gq_ref[0, :BLOCK] = jnp.concatenate([dqr[h][:, :HEAD_DIM] for h in range(HEADS)], axis=1)
        gq_ref[0, BLOCK:] = jnp.concatenate([dqr[h][:, HEAD_DIM:] for h in range(HEADS)], axis=1)

    proj_core()

    with jax.named_scope("grad_keys_values"):
        for off in NEAR:
            got(dkr.at[behind(off)], DK + off)
        pieces = [dkr[h].reshape(TOKENS, 128) for h in range(HEADS)]
        gk_ref[0] = jnp.concatenate([p[:, :HEAD_DIM] for p in pieces], axis=1)
        gv_ref[0] = jnp.concatenate([p[:, HEAD_DIM:] for p in pieces], axis=1)

    with jax.named_scope("grad_proj_end"):
        got(s4b, RF)
        gp_ref[:, theirs] = s4b[...]

    with jax.named_scope("sent"):
        for d in range(1, ny):
            sent(pj_ref.at[:, mine], PY + d)
            sent(s2.at[(y + d) % ny], RY + d)
        for d in range(1, nx):
            sent(pj.at[c, :, x], PX + d)
            sent(s1.at[:, (x + d) % nx], RX + d)
        sent(pj.at[c], PS)
        sent(pp.at[other], RS)
        sent(s4, RF)
        sent(kvp.at[z], KVF)
        sent(xs.at[z], XK)
        for off in range(1, CHIPS):
            zt, zf = ahead(off), behind(off)
            sent(tblme, TBL + off)
            sent(kvp.at[zt], KV + off)
            sent(kv.at[pl.ds(4 * zf + 2 * c, 2)], KVF + off)
            sent(qp.at[zt], QS + off)
            sent(gpk.at[zt], GS + off)
            sent(ats.at[zf], AT + off)
            sent(dqs.at[zf], DQ + off)
            sent(xs.at[zt], XK + off)
            sent(dks.at[zt], DK + off)
            sent(s3, RZ + off)


def attention_grads(nx, ny, q, k, v, go, rb, proj):
    bf, f32 = jnp.bfloat16, jnp.float32
    rows = nx * ny * 16
    hbm = pl.BlockSpec(memory_space=pl.ANY)
    vmem = pl.BlockSpec(memory_space=pltpu.VMEM)
    scratch = [
        pltpu.VMEM((1, TOKENS, WIDTH), bf),
        pltpu.VMEM((1, TOKENS, WIDTH), bf),
        pltpu.VMEM((1, TOKENS, WIDTH), bf),
        pltpu.VMEM((1, TOKENS, WIDTH), bf),
        pltpu.SMEM((1, 2, RANDOM), jnp.int32),
        pltpu.VMEM((16, WIDTH), bf),
        pltpu.VMEM((8, 128), jnp.int32),
        pltpu.VMEM((CHIPS, 8, 128), jnp.int32),
        pltpu.SMEM((CHIPS, 8, 128), jnp.int32),
        pltpu.VMEM((HEADS, 2, BLOCK, 128), bf),
        pltpu.VMEM((BLOCKS, BLOCK, 128), bf),
        pltpu.VMEM((HEADS, BLOCK, 128), bf),
        pltpu.VMEM((CHIPS, BLOCK, 128), bf),
        pltpu.VMEM((HEADS, BLOCK, 128), bf),
        pltpu.VMEM((CHIPS, BLOCK, 128), bf),
        pltpu.VMEM((2, ny, nx, 16, HALF), bf),
        pltpu.VMEM((CHIPS, 2, BLOCK, 8 * BLOCK), bf),
        pltpu.VMEM((BLOCKS, BLOCK, 128), f32),
        pltpu.VMEM((CHIPS * 2 * RANDOM, BLOCK, 128), f32),
        pltpu.VMEM((CHIPS, BLOCK, 128), bf),
        pltpu.VMEM((HEADS, BLOCK, 128), bf),
        pltpu.VMEM((CHIPS, BLOCK, 128), bf),
        pltpu.VMEM((HEADS, BLOCK, 128), bf),
        pltpu.VMEM((CHIPS, 2, BLOCK, 128), bf),
        pltpu.VMEM((CHIPS, 2, BLOCK, 128), bf),
        pltpu.VMEM((CHIPS, 2, BLOCK, 128), bf),
        pltpu.VMEM((HEADS, 2, BLOCK, 128), bf),
        pltpu.VMEM((2, rows, HALF), bf),
        pltpu.VMEM((rows, HALF), bf),
        pltpu.VMEM((ny, nx, 16, HALF), bf),
        pltpu.VMEM((nx, ny, 16, HALF), bf),
        pltpu.VMEM((ny, 16, HALF), bf),
        pltpu.VMEM((ny, 16, HALF), bf),
        pltpu.VMEM((16, HALF), bf),
        pltpu.VMEM((CHIPS, 16, HALF), bf),
        pltpu.VMEM((16, HALF), f32),
        pltpu.VMEM((16, HALF), f32),
        pltpu.SemaphoreType.DMA((SEMS,)),
        pltpu.SemaphoreType.DMA((SEMS,)),
        pltpu.SemaphoreType.DMA((7,)),
    ]
    tokens = jax.ShapeDtypeStruct((1, TOKENS, WIDTH), bf)
    return pl.pallas_call(
        functools.partial(kernel, nx, ny),
        out_shape=[tokens, tokens, tokens, jax.ShapeDtypeStruct((16, WIDTH), f32)],
        in_specs=[hbm] * 6,
        out_specs=[vmem, vmem, vmem, vmem],
        scratch_shapes=scratch,
        compiler_params=pltpu.CompilerParams(
            collective_id=0, has_side_effects=True, vmem_limit_bytes=48 * 1024 * 1024),
        cost_estimate=pl.CostEstimate(
            flops=2 * 500_000_000, bytes_accessed=2_000_000, transcendentals=600_000),
    )(q, k, v, go, rb, proj)


def solution(mesh, nx=4, ny=8):
    tokens = P("dp", "seq", None)
    return jax.shard_map(
        functools.partial(attention_grads, nx, ny),
        mesh=mesh,
        in_specs=(tokens, tokens, tokens, tokens, tokens, P("dp", None)),
        out_specs=(tokens, tokens, tokens, P("dp", None)),
        check_vma=False,
    )
```

```python
import functools

import jax
import jax.numpy as jnp
from jax import lax
from jax.experimental import pallas as pl
from jax.experimental.pallas import tpu as pltpu
from jax.sharding import PartitionSpec as P

HEADS = 8
HEAD_DIM = 64
BLOCK = 64
RANDOM = 3
CHIPS = 8
TOKENS = 128
WIDTH = 512
HALF = 256
BLOCKS = 32
SCALE = HEAD_DIM ** (-0.5)
NEG = -1e30
NEAR = (1, 7, 2, 6, 3, 5, 4)
FAR = (4, 3, 5, 2, 6, 1, 7)
PER = 2
VMEM = 40 * 1024 * 1024

KVF, QS, GS, TBL, PY, PX, PS, AT, DQ, XK, DK, RS, RX, RY, RZ, RF = range(16)
KV, XKR, SEMS = 16, 24, 32
EXP2 = SCALE * 1.4426950408889634


def dot(a, b, dims):
    return lax.dot_general(a, b, (dims, ((), ())), preferred_element_type=jnp.float32)


def halves(a, b):
    return jnp.concatenate([a, b], axis=1)


def kernel(nx, ny, q_hbm, k_hbm, v_hbm, go_hbm, rb_hbm, pj_hbm, gq_ref, gk_ref, gv_ref, gp_ref,
           q_ref, k_ref, v_ref, go_ref, rb_ref, pj_ref,
           tblme, tblv, tbls, kvp, kv, kk, vv, qp, qr, gpk, gr, pj, pst, acc, trand, ats, atr, dqs, dqr,
           xs, xr, dks, dkr, pp, pps, s1, rx, s2, ry, s3, rz, s4, s4b, ssem, rsem, lsem):
    dp = lax.axis_index("dp")
    s = lax.axis_index("seq")
    z, c = s // 2, s % 2
    y, x = dp // nx, dp % nx
    other = 1 - c
    sib = (dp, 2 * z + other)

    def zdev(zt):
        return (dp, 2 * zt + c)

    def xdev(d):
        return (y * nx + (x + d) % nx, s)

    def ydev(d):
        return (((y + d) % ny) * nx + x, s)

    def send(src, dst, sem, dev, arrival=None):
        arrival = sem if arrival is None else arrival
        copy = pltpu.make_async_remote_copy(
            src_ref=src, dst_ref=dst, send_sem=ssem.at[sem], recv_sem=rsem.at[arrival],
            device_id=dev, device_id_type=pl.DeviceIdType.MESH)
        copy.start()

    def got(dst, sem):
        pltpu.make_async_remote_copy(
            src_ref=dst, dst_ref=dst, send_sem=ssem.at[0], recv_sem=rsem.at[sem],
            device_id=sib, device_id_type=pl.DeviceIdType.MESH).wait_recv()

    def sent(src, sem):
        pltpu.make_async_remote_copy(
            src_ref=src, dst_ref=src, send_sem=ssem.at[sem], recv_sem=rsem.at[0],
            device_id=sib, device_id_type=pl.DeviceIdType.MESH).wait_send()

    def ahead(off):
        return (z + off) % CHIPS

    def behind(off):
        return (z + CHIPS - off) % CHIPS

    barrier = pltpu.get_barrier_semaphore()
    partners = [sib] + [zdev(ahead(off)) for off in range(1, CHIPS)]
    partners += [xdev(d) for d in range(1, nx)] + [ydev(d) for d in range(1, ny)]
    for dev in partners:
        pl.semaphore_signal(barrier, inc=1, device_id=dev, device_id_type=pl.DeviceIdType.MESH)

    loads = [pltpu.make_async_copy(a, b, lsem.at[1 + n]) for n, (a, b) in enumerate((
        (pj_hbm, pj_ref), (rb_hbm, rb_ref), (k_hbm, k_ref), (v_hbm, v_ref), (q_hbm, q_ref),
        (go_hbm, go_ref)))]
    for load in loads:
        load.start()

    mine = pl.ds(pl.multiple_of(c * HALF, HALF), HALF)
    theirs = pl.ds(pl.multiple_of(other * HALF, HALF), HALF)

    low = lax.broadcasted_iota(jnp.int32, (BLOCK, 128), 1) < HEAD_DIM

    def swap(a):
        return halves(a[:, HEAD_DIM:], a[:, :HEAD_DIM])

    def fill(source):
        for n in range(2):
            j = 2 * source + n
            pair = kv[j]
            turned = swap(pair)
            kk[j] = jnp.where(low, pair, turned)
            vv[j] = jnp.where(low, turned, pair)

    with jax.named_scope("pack_inputs"):
        loads[0].wait()
        loads[1].wait()
        pj[c, y, x] = pj_ref[:, mine]
        lane = lax.broadcasted_iota(jnp.int32, (8, 128), 1)
        row = jnp.zeros((8, 128), jnp.int32)
        for e in range(2 * RANDOM):
            block = rb_ref[0, e // RANDOM, e % RANDOM]
            own = block // 2
            row = jnp.where(lane == own, e, row)
            row = jnp.where(lane == own + 16 + 16 * (block % 2), 1, row)
            row = jnp.where(lane == 48 + e, block, row)
        tblme[...] = row
        tblv[z] = row
        loads[2].wait()
        loads[3].wait()
        for h in range(HEADS):
            f = slice(h * HEAD_DIM, (h + 1) * HEAD_DIM)
            kvp[h] = halves(k_ref[0, :, f], v_ref[0, :, f]).reshape(2, BLOCK, 128)
        kv[pl.ds(2 * s, 2)] = kvp[z]
        loads[4].wait()
        for h in range(HEADS):
            f = slice(h * HEAD_DIM, (h + 1) * HEAD_DIM)
            qp[h] = halves(q_ref[0, :BLOCK, f], q_ref[0, BLOCK:, f])
        qr[z] = qp[z]
        fill(s)

    with jax.named_scope("barrier"):
        pl.semaphore_wait(barrier, len(partners))

    with jax.named_scope("first_sends"):
        for d in range(1, ny):
            send(pj_ref.at[:, mine], pj.at[c, y, x], PY, ydev(d))
        for off in FAR:
            zt = ahead(off)
            send(kvp.at[zt], kv.at[pl.ds(2 * s, 2)], KV, zdev(zt), KV + off)
        send(kvp.at[z], kv.at[pl.ds(2 * s, 2)], KVF, sib)
        for off in FAR:
            send(tblme, tblv.at[z], TBL, zdev(ahead(off)))
        for off in FAR:
            zt = ahead(off)
            send(qp.at[zt], qr.at[z], QS, zdev(zt))

    acc[...] = jnp.zeros_like(acc)

    with jax.named_scope("proj_rows_y"):
        got(pj.at[c, pl.ds(0, ny - 1), 0], PY)
        for d in range(1, nx):
            send(pj.at[c, :, x], pj.at[c, :, x], PX, xdev(d))

    def forward(off):
        zf = behind(off)
        part = kv.at[pl.ds(4 * zf + 2 * c, 2)]
        got(part, KV + off)
        send(part, part, KVF, sib)
        fill(2 * zf + c)

    with jax.named_scope("forward_a"):
        for off in NEAR[:4]:
            forward(off)

    with jax.named_scope("proj_rows_x"):
        got(pj.at[c, :, pl.ds(0, nx - 1)], PX)
        send(pj.at[c], pj.at[c], PS, sib)

    with jax.named_scope("forward_b"):
        for off in NEAR[4:]:
            forward(off)

    with jax.named_scope("tables"):
        got(tblv.at[pl.ds(0, CHIPS - 1)], TBL)
        table = pltpu.make_async_copy(tblv, tbls, lsem.at[0])
        table.start()
    with jax.named_scope("proj_other"):
        got(pj.at[other], PS)
        loads[5].wait()
    with jax.named_scope("grad_attn"):
        rows = nx * ny * 16
        ga = dot(go_ref[0, :, :HALF], pj[0].reshape(rows, HALF), ((1,), (1,)))
        ga += dot(go_ref[0, :, HALF:], pj[1].reshape(rows, HALF), ((1,), (1,)))
        ga = ga.astype(jnp.bfloat16)
        for h in range(HEADS):
            f = slice(h * HEAD_DIM, (h + 1) * HEAD_DIM)
            gpk[h] = halves(ga[:BLOCK, f], ga[BLOCK:, f])
        gr[z] = gpk[z]
        for off in FAR:
            zt = ahead(off)
            send(gpk.at[zt], gr.at[z], GS, zdev(zt))

    with jax.named_scope("other_core_keys"):
        table.wait()
        got(kv.at[pl.ds(0, 2 * CHIPS)], KVF)
        for k in range(CHIPS):
            fill(2 * k + other)

    high = jnp.logical_not(low)
    none = jnp.zeros((BLOCK, 128), jnp.bfloat16)

    def diagonal(a, b):
        return jnp.concatenate([jnp.where(low, a, none), jnp.where(high, b, none)], axis=0)

    def slots(zs, b):
        i = 4 * zs + 2 * c + b
        fixed = (jnp.maximum(i - 1, 0), i, jnp.minimum(i + 1, BLOCKS - 1), 0, 1)
        return i, fixed, [tbls[zs, 0, 48 + RANDOM * b + n] for n in range(RANDOM)]

    def paired(ref, blocks):
        return jnp.concatenate(
            [jnp.where(low, ref[a], ref[b]) for a, b in zip(*blocks)], axis=0)

    def named(zs):
        return [list(fixed) + ids for _, fixed, ids in (slots(zs, b) for b in range(2))]

    def softmax(zs):
        biases = []
        for b in range(2):
            i, fixed, ids = slots(zs, b)
            valid = [i >= 1, i >= 0, i < BLOCKS - 1, i >= 2, i >= 3]
            for n in range(RANDOM):
                r = ids[n]
                clash = (r == i - 1) | (r == i) | (r == i + 1) | (r <= 1)
                for earlier in ids[:n]:
                    clash = clash | (r == earlier)
                valid.append(jnp.logical_not(clash))
            biases.append([jnp.where(v, 0.0, NEG) for v in valid])
        qf = qr[zs]
        blocks = named(zs)
        scores = dot(paired(kk, blocks), diagonal(qf, qf), ((1,), (1,)))
        scores = jnp.concatenate([
            scores[n * BLOCK:(n + 1) * BLOCK] + jnp.where(low[:1], biases[0][n], biases[1][n])
            for n in range(8)], axis=0)
        top = jnp.max(scores, axis=0, keepdims=True)
        e = jnp.exp2((scores - top) * EXP2)
        prob = (e * (1.0 / jnp.sum(e, axis=0, keepdims=True))).astype(jnp.bfloat16)
        pst[zs] = prob
        out = dot(prob, paired(vv, blocks), ((0,), (0,)))
        ats[zs] = jnp.where(low, out[:BLOCK], out[BLOCK:]).astype(jnp.bfloat16)

    def backward(zs):
        qf, gf = qr[zs], gr[zs]
        blocks = named(zs)
        dprob = dot(paired(vv, blocks), diagonal(gf, gf) * SCALE, ((1,), (1,)))
        low_prob = pst[zs]
        prob = low_prob.astype(jnp.float32)
        delta = jnp.sum(prob * dprob, axis=0, keepdims=True)
        dscore = (prob * (dprob - delta)).astype(jnp.bfloat16)
        out = dot(dscore, paired(kk, blocks), ((0,), (0,)))
        dqs[zs] = jnp.where(low, out[:BLOCK], out[BLOCK:]).astype(jnp.bfloat16)
        wide_low = jnp.concatenate([low] * 8, axis=0)
        sides = (jnp.where(wide_low, dscore, swap(low_prob)),
                 jnp.where(wide_low, swap(dscore), low_prob))
        right = (diagonal(qf, swap(gf)), diagonal(swap(qf), gf))
        terms = [dot(sides[b], right[b], ((1,), (0,))) for b in range(2)]
        return blocks, terms

    def collect(zs, blocks, terms):
        for b in range(2):
            for n in range(5):
                acc[blocks[b][n]] += terms[b][n * BLOCK:(n + 1) * BLOCK]
            for n in range(RANDOM):
                trand[zs * 2 * RANDOM + RANDOM * b + n] = terms[b][(5 + n) * BLOCK:(6 + n) * BLOCK]

    def far(step, n):
        k = step * (PER // 2) + n // 2
        return ahead(CHIPS // 2 - k if n % 2 else (CHIPS // 2 + 1 + k) % CHIPS)

    def wide(ref):
        return ref.astype(jnp.float32)

    with jax.named_scope("queries_wait"):
        got(qr.at[pl.ds(0, CHIPS - 1)], QS)
    with jax.named_scope("softmax"):
        @pl.loop(0, CHIPS // PER)
        def _(step):
            sources = [far(step, n) for n in range(PER)]
            for zs in sources:
                softmax(zs)
            for n, zs in enumerate(sources):
                if n < PER - 2:
                    send(ats.at[zs], atr.at[z], AT, zdev(zs))
                elif n == PER - 1:
                    send(ats.at[zs], atr.at[z], AT, zdev(zs))
                else:
                    @pl.when(step < CHIPS // PER - 1)
                    def _():
                        send(ats.at[zs], atr.at[z], AT, zdev(zs))

        atr[z] = ats[z]

    def partial_proj():
        with jax.named_scope("attn_back"):
            got(atr.at[pl.ds(0, CHIPS - 1)], AT)
        with jax.named_scope("partial_proj"):
            attn = jnp.concatenate([
                jnp.concatenate([atr[h][:, :HEAD_DIM] for h in range(HEADS)], axis=1),
                jnp.concatenate([atr[h][:, HEAD_DIM:] for h in range(HEADS)], axis=1)], axis=0)
            for half in range(2):
                f = slice(half * HALF, (half + 1) * HALF)
                pp[half] = dot(attn, go_ref[0, :, f], ((0,), (0,))).astype(jnp.bfloat16)
            send(pp.at[other], pps, RS, sib)

    def proj_x():
        with jax.named_scope("grad_proj_x"):
            got(pps, RS)
            total = wide(pp[c]) + wide(pps[...])
            s1[...] = total.astype(jnp.bfloat16).reshape(ny, nx, 16, HALF)
            for d in range(1, nx):
                xt = (x + d) % nx
                send(s1.at[:, xt], rx.at[d], RX, xdev(d))

    def proj_y():
        with jax.named_scope("grad_proj_y"):
            total = wide(s1[:, x])
            got(rx.at[pl.ds(1, nx - 1)], RX)
            for d in range(1, nx):
                total += wide(rx[d])
            s2[...] = total.astype(jnp.bfloat16)
            for d in range(1, ny):
                send(s2.at[(y + d) % ny], ry.at[d], RY, ydev(d))

    def proj_z():
        with jax.named_scope("grad_proj_z"):
            total = wide(s2[y])
            got(ry.at[pl.ds(1, ny - 1)], RY)
            for d in range(1, ny):
                total += wide(ry[d])
            s3[...] = total.astype(jnp.bfloat16)
            rz[z] = s3[...]
            for off in FAR:
                send(s3, rz.at[z], RZ, zdev(ahead(off)))

    def proj_core():
        with jax.named_scope("grad_proj_core"):
            got(rz.at[pl.ds(0, CHIPS - 1)], RZ)
            total = wide(rz[0])
            for k in range(1, CHIPS):
                total += wide(rz[k])
            s4[...] = total
            send(s4, s4b, RF, sib)
            gp_ref[:, mine] = total

    with jax.named_scope("grad_attn_wait"):
        got(gr.at[pl.ds(0, CHIPS - 1)], GS)
    with jax.named_scope("gradients"):
        @pl.loop(0, CHIPS // PER)
        def _(step):
            sources = [far(step, n) for n in range(PER)]
            results = [backward(zs) for zs in sources]
            for zs, (blocks, terms) in zip(sources, results):
                collect(zs, blocks, terms)
            for n, zs in enumerate(sources):
                if n < PER - 2:
                    send(dqs.at[zs], dqr.at[z], DQ, zdev(zs))
                elif n == PER - 1:
                    send(dqs.at[zs], dqr.at[z], DQ, zdev(zs))
                else:
                    @pl.when(step < CHIPS // PER - 1)
                    def _():
                        send(dqs.at[zs], dqr.at[z], DQ, zdev(zs))

            pl.when(step == 0)(partial_proj)
            pl.when(step == 1)(proj_x)

        dqr[z] = dqs[z]

    def pull(o):
        parts = [acc[2 * o], acc[2 * o + 1]]
        for zs in range(CHIPS):
            term = trand[zs * 2 * RANDOM + tbls[zs, 0, o]]
            for w in range(2):
                parts[w] += term * tbls[zs, 0, 16 + 16 * w + o].astype(jnp.float32)
        return parts

    with jax.named_scope("other_core_terms"):
        @pl.loop(0, CHIPS)
        def _(step):
            off = (step + 4) % CHIPS
            k = ahead(off)
            parts = pull(2 * k + other)
            for w in range(2):
                xs[k, w] = parts[w].astype(jnp.bfloat16)
            send(xs.at[k], xr.at[k], XK, sib, XKR + off)

    with jax.named_scope("own_terms"):
        @pl.loop(0, CHIPS)
        def _(step):
            off = (step + 4) % CHIPS
            k = ahead(off)
            parts = pull(2 * k + c)
            got(xr.at[k], XKR + off)
            for w in range(2):
                dks[k, w] = (parts[w] + xr[k, w].astype(jnp.float32)).astype(jnp.bfloat16)

            @pl.when(off > 0)
            def _():
                send(dks.at[k], dkr.at[z], DK, zdev(k))

        dkr[z] = dks[z]

    proj_y()
    proj_z()

    with jax.named_scope("grad_queries"):
        got(dqr.at[pl.ds(0, CHIPS - 1)], DQ)
        gq_ref[0, :BLOCK] = jnp.concatenate([dqr[h][:, :HEAD_DIM] for h in range(HEADS)], axis=1)
        gq_ref[0, BLOCK:] = jnp.concatenate([dqr[h][:, HEAD_DIM:] for h in range(HEADS)], axis=1)

    proj_core()

    with jax.named_scope("grad_keys_values"):
        got(dkr.at[pl.ds(0, CHIPS - 1)], DK)
        pieces = [dkr[h].reshape(TOKENS, 128) for h in range(HEADS)]
        gk_ref[0] = jnp.concatenate([p[:, :HEAD_DIM] for p in pieces], axis=1)
        gv_ref[0] = jnp.concatenate([p[:, HEAD_DIM:] for p in pieces], axis=1)

    with jax.named_scope("grad_proj_end"):
        got(s4b, RF)
        gp_ref[:, theirs] = s4b[...]

    with jax.named_scope("sent"):
        rest = pl.ds(0, CHIPS - 1)
        sent(pj.at[0, pl.ds(0, ny - 1), 0], PY)
        sent(pj.at[0, :, pl.ds(0, nx - 1)], PX)
        sent(pj.at[0], PS)
        sent(tblv.at[rest], TBL)
        sent(kvp.at[rest], KV)
        sent(kvp, KVF)
        sent(qp.at[rest], QS)
        sent(gpk.at[rest], GS)
        sent(ats.at[rest], AT)
        sent(dqs.at[rest], DQ)
        sent(xs, XK)
        sent(dks.at[rest], DK)
        sent(pps, RS)
        sent(s1.at[:, pl.ds(0, nx - 1)], RX)
        sent(s2.at[pl.ds(0, ny - 1)], RY)
        sent(rz.at[rest], RZ)
        sent(s4, RF)


def store(*refs):
    count = len(refs) // 2
    copies = [pltpu.make_async_copy(refs[n], refs[count + n], refs[-1].at[n]) for n in range(count)]
    for copy in copies:
        copy.start()
    for copy in copies:
        copy.wait()


def attention_grads(nx, ny, q, k, v, go, rb, proj):
    bf, f32 = jnp.bfloat16, jnp.float32
    rows = nx * ny * 16
    hbm = pl.BlockSpec(memory_space=pltpu.HBM)
    vmem = pl.BlockSpec(memory_space=pltpu.VMEM)
    scratch = [
        pltpu.VMEM((1, TOKENS, WIDTH), bf),
        pltpu.VMEM((1, TOKENS, WIDTH), bf),
        pltpu.VMEM((1, TOKENS, WIDTH), bf),
        pltpu.VMEM((1, TOKENS, WIDTH), bf),
        pltpu.SMEM((1, 2, RANDOM), jnp.int32),
        pltpu.VMEM((16, WIDTH), bf),
        pltpu.VMEM((8, 128), jnp.int32),
        pltpu.VMEM((CHIPS, 8, 128), jnp.int32),
        pltpu.SMEM((CHIPS, 8, 128), jnp.int32),
        pltpu.VMEM((HEADS, 2, BLOCK, 128), bf),
        pltpu.VMEM((BLOCKS, BLOCK, 128), bf),
        pltpu.VMEM((BLOCKS, BLOCK, 128), bf),
        pltpu.VMEM((BLOCKS, BLOCK, 128), bf),
        pltpu.VMEM((HEADS, BLOCK, 128), bf),
        pltpu.VMEM((CHIPS, BLOCK, 128), bf),
        pltpu.VMEM((HEADS, BLOCK, 128), bf),
        pltpu.VMEM((CHIPS, BLOCK, 128), bf),
        pltpu.VMEM((2, ny, nx, 16, HALF), bf),
        pltpu.VMEM((CHIPS, 8 * BLOCK, 128), bf),
        pltpu.VMEM((BLOCKS, BLOCK, 128), f32),
        pltpu.VMEM((CHIPS * 2 * RANDOM, BLOCK, 128), f32),
        pltpu.VMEM((CHIPS, BLOCK, 128), bf),
        pltpu.VMEM((HEADS, BLOCK, 128), bf),
        pltpu.VMEM((CHIPS, BLOCK, 128), bf),
        pltpu.VMEM((HEADS, BLOCK, 128), bf),
        pltpu.VMEM((CHIPS, 2, BLOCK, 128), bf),
        pltpu.VMEM((CHIPS, 2, BLOCK, 128), bf),
        pltpu.VMEM((CHIPS, 2, BLOCK, 128), bf),
        pltpu.VMEM((HEADS, 2, BLOCK, 128), bf),
        pltpu.VMEM((2, rows, HALF), bf),
        pltpu.VMEM((rows, HALF), bf),
        pltpu.VMEM((ny, nx, 16, HALF), bf),
        pltpu.VMEM((nx, ny, 16, HALF), bf),
        pltpu.VMEM((ny, 16, HALF), bf),
        pltpu.VMEM((ny, 16, HALF), bf),
        pltpu.VMEM((16, HALF), bf),
        pltpu.VMEM((CHIPS, 16, HALF), bf),
        pltpu.VMEM((16, HALF), f32),
        pltpu.VMEM((16, HALF), f32),
        pltpu.SemaphoreType.DMA((SEMS,)),
        pltpu.SemaphoreType.DMA((SEMS,)),
        pltpu.SemaphoreType.DMA((7,)),
    ]
    tokens = jax.ShapeDtypeStruct((1, TOKENS, WIDTH), bf)
    shapes = [tokens, tokens, tokens, jax.ShapeDtypeStruct((16, WIDTH), f32)]
    grads = pl.pallas_call(
        functools.partial(kernel, nx, ny),
        out_shape=shapes,
        in_specs=[hbm] * 6,
        out_specs=[vmem, vmem, vmem, vmem],
        scratch_shapes=scratch,
        compiler_params=pltpu.CompilerParams(
            collective_id=0, has_side_effects=True, vmem_limit_bytes=VMEM),
        cost_estimate=pl.CostEstimate(
            flops=2 * 500_000_000, bytes_accessed=2_000_000, transcendentals=600_000),
    )(*[pltpu.with_memory_space_constraint(a, pltpu.HBM) for a in (q, k, v, go, rb, proj)])
    return pl.pallas_call(
        store,
        out_shape=shapes,
        in_specs=[vmem] * 4,
        out_specs=[hbm] * 4,
        scratch_shapes=[pltpu.SemaphoreType.DMA((4,))],
        compiler_params=pltpu.CompilerParams(vmem_limit_bytes=1024 * 1024),
    )(*grads)


def solution(mesh, nx=4, ny=8):
    tokens = P("dp", "seq", None)
    return jax.shard_map(
        functools.partial(attention_grads, nx, ny),
        mesh=mesh,
        in_specs=(tokens, tokens, tokens, tokens, tokens, P("dp", None)),
        out_specs=(tokens, tokens, tokens, P("dp", None)),
        check_vma=False,
    )
```

```python
import functools

import jax
import jax.numpy as jnp
from jax import lax
from jax.experimental import pallas as pl
from jax.experimental.pallas import tpu as pltpu
from jax.sharding import PartitionSpec as P

HEADS = 8
HEAD_DIM = 64
BLOCK = 64
RANDOM = 3
CHIPS = 8
TOKENS = 128
WIDTH = 512
HALF = 256
BLOCKS = 32
SCALE = HEAD_DIM ** (-0.5)
NEG = -1e30
FAR = (4, 3, 5, 2, 6, 1, 7)
PART = 4
VMEM = 40 * 1024 * 1024

KVF, QS, GS, TBL, PY, PX, PS, AT, DQ, XK, DK, RS, RX, RZ = range(14)
KV, XKR, SEMS = 16, 24, 32
EXP2 = SCALE * 1.4426950408889634


def dot(a, b, dims):
    return lax.dot_general(a, b, (dims, ((), ())), preferred_element_type=jnp.float32)


def halves(a, b):
    return jnp.concatenate([a, b], axis=1)


def kernel(nx, ny, q_hbm, k_hbm, v_hbm, go_hbm, rb_hbm, pj_hbm, gq_ref, gk_ref, gv_ref, gp_ref,
           q_ref, k_ref, v_ref, go_ref, rb_ref, pj_ref,
           tblme, tblv, tbls, kvp, kv, kk, vv, qp, qr, gpk, gr, pj, sst, pst, dst, acc, trand, ats, atr, dqs, dqr,
           xs, xr, dks, dkr, pp, pps, s1, rx, s3, rz, ssem, rsem, lsem):
    dp = lax.axis_index("dp")
    s = lax.axis_index("seq")
    z, c = s // 2, s % 2
    y, x = dp // nx, dp % nx
    other = 1 - c
    sib = (dp, 2 * z + other)

    def zdev(zt):
        return (dp, 2 * zt + c)

    def xdev(d):
        return (y * nx + (x + d) % nx, s)

    def ydev(d):
        return (((y + d) % ny) * nx + x, s)

    def send(src, dst, sem, dev, arrival=None):
        arrival = sem if arrival is None else arrival
        copy = pltpu.make_async_remote_copy(
            src_ref=src, dst_ref=dst, send_sem=ssem.at[sem], recv_sem=rsem.at[arrival],
            device_id=dev, device_id_type=pl.DeviceIdType.MESH)
        copy.start()

    def got(dst, sem):
        pltpu.make_async_remote_copy(
            src_ref=dst, dst_ref=dst, send_sem=ssem.at[0], recv_sem=rsem.at[sem],
            device_id=sib, device_id_type=pl.DeviceIdType.MESH).wait_recv()

    def sent(src, sem):
        pltpu.make_async_remote_copy(
            src_ref=src, dst_ref=src, send_sem=ssem.at[sem], recv_sem=rsem.at[0],
            device_id=sib, device_id_type=pl.DeviceIdType.MESH).wait_send()

    def ahead(off):
        return (z + off) % CHIPS

    def behind(off):
        return (z + CHIPS - off) % CHIPS

    barrier = pltpu.get_barrier_semaphore()
    partners = [zdev(ahead(off)) for off in FAR] + [ydev(d) for d in sorted(
        range(1, ny), key=lambda d: -min(d, ny - d))]
    partners += [xdev(d) for d in range(1, nx)] + [sib]
    for dev in partners:
        pl.semaphore_signal(barrier, inc=1, device_id=dev, device_id_type=pl.DeviceIdType.MESH)

    loads = [pltpu.make_async_copy(a, b, lsem.at[1 + n]) for n, (a, b) in enumerate((
        (pj_hbm, pj_ref), (rb_hbm, rb_ref), (k_hbm, k_ref), (v_hbm, v_ref), (q_hbm, q_ref),
        (go_hbm, go_ref)))]
    for load in loads:
        load.start()

    mine = pl.ds(pl.multiple_of(c * HALF, HALF), HALF)
    theirs = pl.ds(pl.multiple_of(other * HALF, HALF), HALF)

    low = lax.broadcasted_iota(jnp.int32, (BLOCK, 128), 1) < HEAD_DIM

    def swap(a):
        return halves(a[:, HEAD_DIM:], a[:, :HEAD_DIM])

    def fill(source):
        for n in range(2):
            j = 2 * source + n
            pair = kv[j]
            turned = swap(pair)
            kk[j] = jnp.where(low, pair, turned)
            vv[j] = jnp.where(low, turned, pair)

    with jax.named_scope("pack_inputs"):
        loads[0].wait()
        loads[1].wait()
        pj[c, y, x] = pj_ref[:, mine]
        lane = lax.broadcasted_iota(jnp.int32, (8, 128), 1)
        row = jnp.zeros((8, 128), jnp.int32)
        for e in range(2 * RANDOM):
            block = rb_ref[0, e // RANDOM, e % RANDOM]
            own = block // 2
            row = jnp.where(lane == own, e, row)
            row = jnp.where(lane == own + 16 + 16 * (block % 2), 1, row)
            row = jnp.where(lane == 48 + e, block, row)
        tblme[...] = row
        tblv[z] = row
        loads[2].wait()
        loads[3].wait()
        for h in range(HEADS):
            f = slice(h * HEAD_DIM, (h + 1) * HEAD_DIM)
            kvp[h] = halves(k_ref[0, :, f], v_ref[0, :, f]).reshape(2, BLOCK, 128)
        kv[pl.ds(2 * s, 2)] = kvp[z]
        loads[4].wait()
        for h in range(HEADS):
            f = slice(h * HEAD_DIM, (h + 1) * HEAD_DIM)
            qp[h] = halves(q_ref[0, :BLOCK, f], q_ref[0, BLOCK:, f])
        qr[z] = qp[z]
        fill(s)

    with jax.named_scope("barrier"):
        pl.semaphore_wait(barrier, len(partners))

    with jax.named_scope("first_sends"):
        for d in range(1, ny):
            send(pj_ref.at[:, mine], pj.at[c, y, x], PY, ydev(d))
        for off in FAR:
            send(tblme, tblv.at[z], TBL, zdev(ahead(off)))
        for off in FAR:
            zt = ahead(off)
            send(kvp.at[zt], kv.at[pl.ds(2 * s, 2)], KV, zdev(zt), KV + off)
        send(kvp.at[z], kv.at[pl.ds(2 * s, 2)], KVF, sib)
        for off in FAR:
            zt = ahead(off)
            send(qp.at[zt], qr.at[z], QS, zdev(zt))

    acc[...] = jnp.zeros_like(acc)

    with jax.named_scope("proj_rows_y"):
        got(pj.at[c, pl.ds(0, ny - 1), 0], PY)
        for d in range(1, nx):
            send(pj.at[c, :, x], pj.at[c, :, x], PX, xdev(d))

    with jax.named_scope("tables"):
        got(tblv.at[pl.ds(0, CHIPS - 1)], TBL)
        table = pltpu.make_async_copy(tblv, tbls, lsem.at[0])
        table.start()
    def forward(off):
        zf = behind(off)
        part = kv.at[pl.ds(4 * zf + 2 * c, 2)]
        got(part, KV + off)
        send(part, part, KVF, sib)
        fill(2 * zf + c)

    with jax.named_scope("forward"):
        for off in FAR:
            forward(off)

    with jax.named_scope("proj_rows_x"):
        got(pj.at[c, :, pl.ds(0, nx - 1)], PX)
        send(pj.at[c], pj.at[c], PS, sib)

    with jax.named_scope("proj_other"):
        got(pj.at[other], PS)
        loads[5].wait()
    with jax.named_scope("grad_attn"):
        rows = nx * ny * 16
        ga = dot(go_ref[0, :, :HALF], pj[0].reshape(rows, HALF), ((1,), (1,)))
        ga += dot(go_ref[0, :, HALF:], pj[1].reshape(rows, HALF), ((1,), (1,)))
        ga = ga.astype(jnp.bfloat16)
        for h in range(HEADS):
            f = slice(h * HEAD_DIM, (h + 1) * HEAD_DIM)
            gpk[h] = halves(ga[:BLOCK, f], ga[BLOCK:, f])
        gr[z] = gpk[z]
        for off in FAR:
            zt = ahead(off)
            send(gpk.at[zt], gr.at[z], GS, zdev(zt))

    with jax.named_scope("other_core_keys"):
        table.wait()
        got(kv.at[pl.ds(0, 2 * CHIPS)], KVF)
        for k in range(CHIPS):
            fill(2 * k + other)

    high = jnp.logical_not(low)
    none = jnp.zeros((BLOCK, 128), jnp.bfloat16)

    def diagonal(a, b):
        return jnp.concatenate([jnp.where(low, a, none), jnp.where(high, b, none)], axis=0)

    def slots(zs, b):
        i = 4 * zs + 2 * c + b
        fixed = (jnp.maximum(i - 1, 0), i, jnp.minimum(i + 1, BLOCKS - 1), 0, 1)
        return i, fixed, [tbls[zs, 0, 48 + RANDOM * b + n] for n in range(RANDOM)]

    def paired(ref, blocks):
        return jnp.concatenate(
            [jnp.where(low, ref[a], ref[b]) for a, b in zip(*blocks)], axis=0)

    def named(zs):
        return [list(fixed) + ids for _, fixed, ids in (slots(zs, b) for b in range(2))]

    def biases(zs):
        both = []
        for b in range(2):
            i, fixed, ids = slots(zs, b)
            valid = [i >= 1, i >= 0, i < BLOCKS - 1, i >= 2, i >= 3]
            for n in range(RANDOM):
                r = ids[n]
                clash = (r == i - 1) | (r == i) | (r == i + 1) | (r <= 1)
                for earlier in ids[:n]:
                    clash = clash | (r == earlier)
                valid.append(jnp.logical_not(clash))
            both.append([jnp.where(v, 0.0, NEG) for v in valid])
        return both

    def block(a, n):
        return a[n * BLOCK:(n + 1) * BLOCK]

    def fold(out):
        return jnp.where(low, block(out, 0), block(out, 1)).astype(jnp.bfloat16)

    def scored(zs):
        bias = biases(zs)
        scores = dot(paired(kk, named(zs)), diagonal(qr[zs], qr[zs]), ((1,), (1,)))
        sst[zs] = jnp.concatenate([
            block(scores, n) + jnp.where(low[:1], bias[0][n], bias[1][n]) for n in range(8)], axis=0)

    def softmax(zs):
        scores = sst[zs]
        top = jnp.max(scores, axis=0, keepdims=True)
        e = jnp.exp2((scores - top) * EXP2)
        pst[zs] = (e * (1.0 / jnp.sum(e, axis=0, keepdims=True))).astype(jnp.bfloat16)

    def attended(zs):
        ats[zs] = fold(dot(pst[zs], paired(vv, named(zs)), ((0,), (0,))))

    def score_grads(zs):
        gf = gr[zs]
        dprob = dot(paired(vv, named(zs)), diagonal(gf, gf) * SCALE, ((1,), (1,)))
        prob = pst[zs].astype(jnp.float32)
        delta = jnp.sum(prob * dprob, axis=0, keepdims=True)
        dst[zs] = (prob * (dprob - delta)).astype(jnp.bfloat16)

    def query_grads(zs):
        dqs[zs] = fold(dot(dst[zs], paired(kk, named(zs)), ((0,), (0,))))

    def block_terms(zs):
        qf, gf = qr[zs], gr[zs]
        prob, dscore = pst[zs], dst[zs]
        left = jnp.concatenate([low] * 8, axis=0)
        first = dot(jnp.where(left, dscore, swap(prob)), diagonal(qf, swap(gf)), ((1,), (0,)))
        second = dot(jnp.where(left, swap(dscore), prob), diagonal(swap(qf), gf), ((1,), (0,)))
        return first, second

    def collect(zs, first, second):
        blocks = named(zs)
        acc[blocks[0][0]] += block(first, 0)
        acc[blocks[0][1]] += block(first, 1) + block(second, 0)
        acc[blocks[1][1]] += block(first, 2) + block(second, 1)
        acc[blocks[1][2]] += block(second, 2)
        for n in range(2):
            acc[n] += block(first, 3 + n) + block(second, 3 + n)
        for b, terms in enumerate((first, second)):
            for n in range(RANDOM):
                trand[zs * 2 * RANDOM + RANDOM * b + n] = block(terms, 5 + n)

    def wide(ref):
        return ref.astype(jnp.float32)

    def partial_proj():
        with jax.named_scope("attn_back"):
            got(atr.at[pl.ds(0, CHIPS - 1)], AT)
        with jax.named_scope("partial_proj"):
            attn = jnp.concatenate([
                jnp.concatenate([atr[h][:, :HEAD_DIM] for h in range(HEADS)], axis=1),
                jnp.concatenate([atr[h][:, HEAD_DIM:] for h in range(HEADS)], axis=1)], axis=0)
            pp[1] = dot(attn, go_ref[0, :, theirs], ((0,), (0,))).astype(jnp.bfloat16)
            send(pp.at[1], pps, RS, sib)
            pp[0] = dot(attn, go_ref[0, :, mine], ((0,), (0,))).astype(jnp.bfloat16)

    def proj_xy():
        with jax.named_scope("grad_proj_core"):
            got(pps, RS)
            total = wide(pp[0]) + wide(pps[...])
            s1[...] = total.astype(jnp.bfloat16).reshape(ny * nx, 16, HALF)
            rx[dp] = s1[dp]
            for dy in sorted(range(ny), key=lambda d: -min(d, ny - d)):
                for dx in sorted(range(nx), key=lambda d: -min(d, nx - d)):
                    if dx or dy:
                        target = ((y + dy) % ny) * nx + (x + dx) % nx
                        send(s1.at[target], rx.at[dp], RX, (target, s))

    def proj_z():
        with jax.named_scope("grad_proj_xy"):
            got(rx.at[pl.ds(0, ny * nx - 1)], RX)
            total = wide(rx[0])
            for d in range(1, ny * nx):
                total += wide(rx[d])
            s3[...] = total.astype(jnp.bfloat16)
            rz[s] = s3[...]
            for off in FAR:
                send(s3, rz.at[s], RZ, zdev(ahead(off)))
                send(s3, rz.at[s], RZ, (dp, 2 * ahead(off) + other))
            send(s3, rz.at[s], RZ, sib)

    def proj_end():
        with jax.named_scope("grad_proj_z"):
            got(rz.at[pl.ds(0, 2 * CHIPS - 1)], RZ)
            for half in range(2):
                total = wide(rz[half])
                for k in range(1, CHIPS):
                    total += wide(rz[2 * k + half])
                gp_ref[:, half * HALF:(half + 1) * HALF] = total

    with jax.named_scope("queries_wait"):
        got(qr.at[pl.ds(0, CHIPS - 1)], QS)
    with jax.named_scope("scores"):
        for zs in range(CHIPS):
            scored(zs)

    with jax.named_scope("softmax"):
        @pl.loop(0, CHIPS // PART)
        def _(step):
            for n in range(PART):
                softmax(step * PART + n)
    with jax.named_scope("attend"):
        for zs in range(CHIPS):
            attended(zs)
        atr[z] = ats[z]
        for off in FAR:
            send(ats.at[ahead(off)], atr.at[z], AT, zdev(ahead(off)))

    with jax.named_scope("grad_attn_wait"):
        got(gr.at[pl.ds(0, CHIPS - 1)], GS)
    with jax.named_scope("score_grads"):
        for zs in range(CHIPS):
            score_grads(zs)
    with jax.named_scope("query_grads"):
        for zs in range(CHIPS):
            query_grads(zs)
        dqr[z] = dqs[z]
        for off in FAR:
            send(dqs.at[ahead(off)], dqr.at[z], DQ, zdev(ahead(off)))
    with jax.named_scope("block_terms"):
        @pl.loop(0, CHIPS // PART)
        def _(step):
            results = [block_terms(step * PART + n) for n in range(PART)]
            for n in range(PART):
                collect(step * PART + n, *results[n])
            pl.when(step == 0)(partial_proj)

    def pull(o):
        parts = [acc[2 * o], acc[2 * o + 1]]
        for zs in range(CHIPS):
            term = trand[zs * 2 * RANDOM + tbls[zs, 0, o]]
            for w in range(2):
                parts[w] += term * tbls[zs, 0, 16 + 16 * w + o].astype(jnp.float32)
        return parts

    with jax.named_scope("other_core_terms"):
        @pl.loop(0, CHIPS)
        def _(step):
            off = (step + 4) % CHIPS
            k = ahead(off)
            parts = pull(2 * k + other)
            for w in range(2):
                xs[k, w] = parts[w].astype(jnp.bfloat16)
            send(xs.at[k], xr.at[k], XK, sib, XKR + off)

    proj_xy()

    with jax.named_scope("own_terms"):
        @pl.loop(0, CHIPS)
        def _(step):
            off = (step + 4) % CHIPS
            k = ahead(off)
            parts = pull(2 * k + c)
            got(xr.at[k], XKR + off)
            for w in range(2):
                dks[k, w] = (parts[w] + xr[k, w].astype(jnp.float32)).astype(jnp.bfloat16)

            @pl.when(off > 0)
            def _():
                send(dks.at[k], dkr.at[z], DK, zdev(k))

        dkr[z] = dks[z]

    proj_z()

    with jax.named_scope("grad_queries"):
        got(dqr.at[pl.ds(0, CHIPS - 1)], DQ)
        gq_ref[0, :BLOCK] = jnp.concatenate([dqr[h][:, :HEAD_DIM] for h in range(HEADS)], axis=1)
        gq_ref[0, BLOCK:] = jnp.concatenate([dqr[h][:, HEAD_DIM:] for h in range(HEADS)], axis=1)

    with jax.named_scope("grad_keys_values"):
        got(dkr.at[pl.ds(0, CHIPS - 1)], DK)
        pieces = [dkr[h].reshape(TOKENS, 128) for h in range(HEADS)]
        gk_ref[0] = jnp.concatenate([p[:, :HEAD_DIM] for p in pieces], axis=1)
        gv_ref[0] = jnp.concatenate([p[:, HEAD_DIM:] for p in pieces], axis=1)

    proj_end()

    with jax.named_scope("sent"):
        rest = pl.ds(0, CHIPS - 1)
        sent(pj.at[0, pl.ds(0, ny - 1), 0], PY)
        sent(pj.at[0, :, pl.ds(0, nx - 1)], PX)
        sent(pj.at[0], PS)
        sent(tblv.at[rest], TBL)
        sent(kvp.at[rest], KV)
        sent(kvp, KVF)
        sent(qp.at[rest], QS)
        sent(gpk.at[rest], GS)
        sent(ats.at[rest], AT)
        sent(dqs.at[rest], DQ)
        sent(xs, XK)
        sent(dks.at[rest], DK)
        sent(pps, RS)
        sent(rx.at[pl.ds(0, ny * nx - 1)], RX)
        sent(rz.at[pl.ds(0, 2 * CHIPS - 1)], RZ)


def store(*refs):
    count = len(refs) // 2
    copies = [pltpu.make_async_copy(refs[n], refs[count + n], refs[-1].at[n]) for n in range(count)]
    for copy in copies:
        copy.start()
    for copy in copies:
        copy.wait()


def attention_grads(nx, ny, q, k, v, go, rb, proj):
    bf, f32 = jnp.bfloat16, jnp.float32
    rows = nx * ny * 16
    hbm = pl.BlockSpec(memory_space=pltpu.HBM)
    vmem = pl.BlockSpec(memory_space=pltpu.VMEM)
    scratch = [
        pltpu.VMEM((1, TOKENS, WIDTH), bf),
        pltpu.VMEM((1, TOKENS, WIDTH), bf),
        pltpu.VMEM((1, TOKENS, WIDTH), bf),
        pltpu.VMEM((1, TOKENS, WIDTH), bf),
        pltpu.SMEM((1, 2, RANDOM), jnp.int32),
        pltpu.VMEM((16, WIDTH), bf),
        pltpu.VMEM((8, 128), jnp.int32),
        pltpu.VMEM((CHIPS, 8, 128), jnp.int32),
        pltpu.SMEM((CHIPS, 8, 128), jnp.int32),
        pltpu.VMEM((HEADS, 2, BLOCK, 128), bf),
        pltpu.VMEM((BLOCKS, BLOCK, 128), bf),
        pltpu.VMEM((BLOCKS, BLOCK, 128), bf),
        pltpu.VMEM((BLOCKS, BLOCK, 128), bf),
        pltpu.VMEM((HEADS, BLOCK, 128), bf),
        pltpu.VMEM((CHIPS, BLOCK, 128), bf),
        pltpu.VMEM((HEADS, BLOCK, 128), bf),
        pltpu.VMEM((CHIPS, BLOCK, 128), bf),
        pltpu.VMEM((2, ny, nx, 16, HALF), bf),
        pltpu.VMEM((CHIPS, 8 * BLOCK, 128), f32),
        pltpu.VMEM((CHIPS, 8 * BLOCK, 128), bf),
        pltpu.VMEM((CHIPS, 8 * BLOCK, 128), bf),
        pltpu.VMEM((BLOCKS, BLOCK, 128), f32),
        pltpu.VMEM((CHIPS * 2 * RANDOM, BLOCK, 128), f32),
        pltpu.VMEM((CHIPS, BLOCK, 128), bf),
        pltpu.VMEM((HEADS, BLOCK, 128), bf),
        pltpu.VMEM((CHIPS, BLOCK, 128), bf),
        pltpu.VMEM((HEADS, BLOCK, 128), bf),
        pltpu.VMEM((CHIPS, 2, BLOCK, 128), bf),
        pltpu.VMEM((CHIPS, 2, BLOCK, 128), bf),
        pltpu.VMEM((CHIPS, 2, BLOCK, 128), bf),
        pltpu.VMEM((HEADS, 2, BLOCK, 128), bf),
        pltpu.VMEM((2, rows, HALF), bf),
        pltpu.VMEM((rows, HALF), bf),
        pltpu.VMEM((ny * nx, 16, HALF), bf),
        pltpu.VMEM((ny * nx, 16, HALF), bf),
        pltpu.VMEM((16, HALF), bf),
        pltpu.VMEM((2 * CHIPS, 16, HALF), bf),
        pltpu.SemaphoreType.DMA((SEMS,)),
        pltpu.SemaphoreType.DMA((SEMS,)),
        pltpu.SemaphoreType.DMA((7,)),
    ]
    tokens = jax.ShapeDtypeStruct((1, TOKENS, WIDTH), bf)
    shapes = [tokens, tokens, tokens, jax.ShapeDtypeStruct((16, WIDTH), f32)]
    grads = pl.pallas_call(
        functools.partial(kernel, nx, ny),
        out_shape=shapes,
        in_specs=[hbm] * 6,
        out_specs=[vmem, vmem, vmem, vmem],
        scratch_shapes=scratch,
        compiler_params=pltpu.CompilerParams(
            collective_id=0, has_side_effects=True, vmem_limit_bytes=VMEM),
        cost_estimate=pl.CostEstimate(
            flops=2 * 500_000_000, bytes_accessed=2_000_000, transcendentals=600_000),
    )(*[pltpu.with_memory_space_constraint(a, pltpu.HBM) for a in (q, k, v, go, rb, proj)])
    return pl.pallas_call(
        store,
        out_shape=shapes,
        in_specs=[vmem] * 4,
        out_specs=[hbm] * 4,
        scratch_shapes=[pltpu.SemaphoreType.DMA((4,))],
        compiler_params=pltpu.CompilerParams(vmem_limit_bytes=1024 * 1024),
    )(*grads)


def solution(mesh, nx=4, ny=8):
    tokens = P("dp", "seq", None)
    return jax.shard_map(
        functools.partial(attention_grads, nx, ny),
        mesh=mesh,
        in_specs=(tokens, tokens, tokens, tokens, tokens, P("dp", None)),
        out_specs=(tokens, tokens, tokens, P("dp", None)),
        check_vma=False,
    )
```

```python
import functools

import jax
import jax.numpy as jnp
from jax import lax
from jax.experimental import pallas as pl
from jax.experimental.pallas import tpu as pltpu
from jax.sharding import PartitionSpec as P

HEADS = 8
HEAD_DIM = 64
BLOCK = 64
RANDOM = 3
CHIPS = 8
TOKENS = 128
WIDTH = 512
HALF = 256
BLOCKS = 32
SCALE = HEAD_DIM ** (-0.5)
NEG = -1e30
FAR = (4, 3, 5, 2, 6, 1, 7)
PART = 4
VMEM = 40 * 1024 * 1024

KVF, QS, GS, TBL, PY, PX, PS, AT, DQ, XK, DK, RS, RX, RZ, KVS = range(15)
SENDS = 15
KV, XKR, RECVS = 16, 24, 32
EXP2 = SCALE * 1.4426950408889634


def dot(a, b, dims):
    return lax.dot_general(a, b, (dims, ((), ())), preferred_element_type=jnp.float32)


def halves(a, b):
    return jnp.concatenate([a, b], axis=1)


def kernel(nx, ny, q_hbm, k_hbm, v_hbm, go_hbm, rb_hbm, pj_hbm, gq_ref, gk_ref, gv_ref, gp_ref,
           q_ref, k_ref, v_ref, go_ref, rb_ref, pj_ref,
           tblme, tblv, tbls, kvp, kv, kk, vv, qp, qr, gpk, gr, pj, sst, pst, dst, acc, trand, ats, atr, dqs, dqr,
           xs, xr, dks, dkr, pp, pps, s1, rx, s3, rz, ssem, rsem, lsem):
    dp = lax.axis_index("dp")
    s = lax.axis_index("seq")
    z, c = s // 2, s % 2
    y, x = dp // nx, dp % nx
    other = 1 - c
    sib = (dp, 2 * z + other)

    def zdev(zt):
        return (dp, 2 * zt + c)

    def xdev(d):
        return (y * nx + (x + d) % nx, s)

    def ydev(d):
        return (((y + d) % ny) * nx + x, s)

    def send(src, dst, sem, dev, arrival=None):
        arrival = sem if arrival is None else arrival
        copy = pltpu.make_async_remote_copy(
            src_ref=src, dst_ref=dst, send_sem=ssem.at[sem], recv_sem=rsem.at[arrival],
            device_id=dev, device_id_type=pl.DeviceIdType.MESH)
        copy.start()

    def got(dst, sem):
        pltpu.make_async_remote_copy(
            src_ref=dst, dst_ref=dst, send_sem=ssem.at[0], recv_sem=rsem.at[sem],
            device_id=sib, device_id_type=pl.DeviceIdType.MESH).wait_recv()

    def sent(src, sem):
        pltpu.make_async_remote_copy(
            src_ref=src, dst_ref=src, send_sem=ssem.at[sem], recv_sem=rsem.at[0],
            device_id=sib, device_id_type=pl.DeviceIdType.MESH).wait_send()

    def ahead(off):
        return (z + off) % CHIPS

    def behind(off):
        return (z + CHIPS - off) % CHIPS

    barrier = pltpu.get_barrier_semaphore()
    hops = [(min(off, CHIPS - off), zdev(ahead(off))) for off in range(1, CHIPS)]
    hops += [(min(d, ny - d), ydev(d)) for d in range(1, ny)]
    hops += [(min(d, nx - d), xdev(d)) for d in range(1, nx)] + [(0, sib)]
    partners = [dev for _, dev in sorted(hops, key=lambda item: -item[0])]
    for dev in partners:
        pl.semaphore_signal(barrier, inc=1, device_id=dev, device_id_type=pl.DeviceIdType.MESH)

    loads = [pltpu.make_async_copy(a, b, lsem.at[1 + n]) for n, (a, b) in enumerate((
        (pj_hbm, pj_ref), (rb_hbm, rb_ref), (k_hbm, k_ref), (v_hbm, v_ref), (q_hbm, q_ref),
        (go_hbm, go_ref)))]
    for load in loads:
        load.start()

    mine = pl.ds(pl.multiple_of(c * HALF, HALF), HALF)
    theirs = pl.ds(pl.multiple_of(other * HALF, HALF), HALF)

    low = lax.broadcasted_iota(jnp.int32, (BLOCK, 128), 1) < HEAD_DIM

    def swap(a):
        return halves(a[:, HEAD_DIM:], a[:, :HEAD_DIM])

    def fill(source):
        for n in range(2):
            j = 2 * source + n
            pair = kv[j]
            turned = swap(pair)
            kk[j] = jnp.where(low, pair, turned)
            vv[j] = jnp.where(low, turned, pair)

    with jax.named_scope("pack_inputs"):
        loads[0].wait()
        loads[1].wait()
        pj[c, y, x] = pj_ref[:, mine]
        lane = lax.broadcasted_iota(jnp.int32, (8, 128), 1)
        row = jnp.zeros((8, 128), jnp.int32)
        for e in range(2 * RANDOM):
            block = rb_ref[0, e // RANDOM, e % RANDOM]
            own = block // 2
            row = jnp.where(lane == own, e, row)
            row = jnp.where(lane == own + 16 + 16 * (block % 2), 1, row)
            row = jnp.where(lane == 48 + e, block, row)
        tblme[...] = row
        tblv[z] = row
        loads[2].wait()
        loads[3].wait()
        for h in range(HEADS):
            f = slice(h * HEAD_DIM, (h + 1) * HEAD_DIM)
            kvp[h] = halves(k_ref[0, :, f], v_ref[0, :, f]).reshape(2, BLOCK, 128)
        kv[pl.ds(2 * s, 2)] = kvp[z]
        loads[4].wait()
        for h in range(HEADS):
            f = slice(h * HEAD_DIM, (h + 1) * HEAD_DIM)
            qp[h] = halves(q_ref[0, :BLOCK, f], q_ref[0, BLOCK:, f])
        qr[z] = qp[z]
        fill(s)

    with jax.named_scope("barrier"):
        pl.semaphore_wait(barrier, len(partners))

    with jax.named_scope("first_sends"):
        for d in range(1, ny):
            send(pj_ref.at[:, mine], pj.at[c, y, x], PY, ydev(d))
        for off in FAR:
            send(tblme, tblv.at[z], TBL, zdev(ahead(off)))
        for off in FAR:
            zt = ahead(off)
            send(kvp.at[zt], kv.at[pl.ds(2 * s, 2)], KVS, zdev(zt), KV + off)
        send(kvp.at[z], kv.at[pl.ds(2 * s, 2)], KVF, sib)
        for off in FAR:
            zt = ahead(off)
            send(qp.at[zt], qr.at[z], QS, zdev(zt))

    acc[...] = jnp.zeros_like(acc)

    with jax.named_scope("proj_rows_y"):
        got(pj.at[c, pl.ds(0, ny - 1), 0], PY)
        for d in range(1, nx):
            send(pj.at[c, :, x], pj.at[c, :, x], PX, xdev(d))

    with jax.named_scope("tables"):
        got(tblv.at[pl.ds(0, CHIPS - 1)], TBL)
        table = pltpu.make_async_copy(tblv, tbls, lsem.at[0])
        table.start()
    def forward(off):
        zf = behind(off)
        part = kv.at[pl.ds(4 * zf + 2 * c, 2)]
        got(part, KV + off)
        send(part, part, KVF, sib)
        fill(2 * zf + c)

    with jax.named_scope("forward"):
        for off in FAR:
            forward(off)

    with jax.named_scope("proj_rows_x"):
        got(pj.at[c, :, pl.ds(0, nx - 1)], PX)
        send(pj.at[c], pj.at[c], PS, sib)

    with jax.named_scope("proj_other"):
        got(pj.at[other], PS)
        loads[5].wait()
    with jax.named_scope("grad_attn"):
        rows = nx * ny * 16
        ga = dot(go_ref[0, :, :HALF], pj[0].reshape(rows, HALF), ((1,), (1,)))
        ga += dot(go_ref[0, :, HALF:], pj[1].reshape(rows, HALF), ((1,), (1,)))
        ga = ga.astype(jnp.bfloat16)
        for h in range(HEADS):
            f = slice(h * HEAD_DIM, (h + 1) * HEAD_DIM)
            gpk[h] = halves(ga[:BLOCK, f], ga[BLOCK:, f])
        gr[z] = gpk[z]
        for off in FAR:
            zt = ahead(off)
            send(gpk.at[zt], gr.at[z], GS, zdev(zt))

    with jax.named_scope("other_core_keys"):
        table.wait()
        got(kv.at[pl.ds(0, 2 * CHIPS)], KVF)
        for k in range(CHIPS):
            fill(2 * k + other)

    high = jnp.logical_not(low)
    none = jnp.zeros((BLOCK, 128), jnp.bfloat16)

    def diagonal(a, b):
        return jnp.concatenate([jnp.where(low, a, none), jnp.where(high, b, none)], axis=0)

    def slots(zs, b):
        i = 4 * zs + 2 * c + b
        fixed = (jnp.maximum(i - 1, 0), i, jnp.minimum(i + 1, BLOCKS - 1), 0, 1)
        return i, fixed, [tbls[zs, 0, 48 + RANDOM * b + n] for n in range(RANDOM)]

    def paired(ref, blocks):
        return jnp.concatenate(
            [jnp.where(low, ref[a], ref[b]) for a, b in zip(*blocks)], axis=0)

    def named(zs):
        return [list(fixed) + ids for _, fixed, ids in (slots(zs, b) for b in range(2))]

    def biases(zs):
        both = []
        for b in range(2):
            i, fixed, ids = slots(zs, b)
            valid = [i >= 1, i >= 0, i < BLOCKS - 1, i >= 2, i >= 3]
            for n in range(RANDOM):
                r = ids[n]
                clash = (r == i - 1) | (r == i) | (r == i + 1) | (r <= 1)
                for earlier in ids[:n]:
                    clash = clash | (r == earlier)
                valid.append(jnp.logical_not(clash))
            both.append([jnp.where(v, 0.0, NEG) for v in valid])
        return both

    def block(a, n):
        return a[n * BLOCK:(n + 1) * BLOCK]

    def fold(out):
        return jnp.where(low, block(out, 0), block(out, 1)).astype(jnp.bfloat16)

    def scored(zs):
        bias = biases(zs)
        scores = dot(paired(kk, named(zs)), diagonal(qr[zs], qr[zs]), ((1,), (1,)))
        sst[zs] = jnp.concatenate([
            block(scores, n) + jnp.where(low[:1], bias[0][n], bias[1][n]) for n in range(8)], axis=0)

    def softmax(zs):
        scores = sst[zs]
        top = jnp.max(scores, axis=0, keepdims=True)
        e = jnp.exp2((scores - top) * EXP2)
        pst[zs] = (e * (1.0 / jnp.sum(e, axis=0, keepdims=True))).astype(jnp.bfloat16)

    def attended(zs):
        ats[zs] = fold(dot(pst[zs], paired(vv, named(zs)), ((0,), (0,))))

    def score_grads(zs):
        gf = gr[zs]
        dprob = dot(paired(vv, named(zs)), diagonal(gf, gf) * SCALE, ((1,), (1,)))
        prob = pst[zs].astype(jnp.float32)
        delta = jnp.sum(prob * dprob, axis=0, keepdims=True)
        dst[zs] = (prob * (dprob - delta)).astype(jnp.bfloat16)

    def query_grads(zs):
        dqs[zs] = fold(dot(dst[zs], paired(kk, named(zs)), ((0,), (0,))))

    def block_terms(zs):
        qf, gf = qr[zs], gr[zs]
        prob, dscore = pst[zs], dst[zs]
        left = jnp.concatenate([low] * 8, axis=0)
        first = dot(jnp.where(left, dscore, swap(prob)), diagonal(qf, swap(gf)), ((1,), (0,)))
        second = dot(jnp.where(left, swap(dscore), prob), diagonal(swap(qf), gf), ((1,), (0,)))
        return first, second

    def collect(zs, first, second):
        blocks = named(zs)
        acc[blocks[0][0]] += block(first, 0)
        acc[blocks[0][1]] += block(first, 1) + block(second, 0)
        acc[blocks[1][1]] += block(first, 2) + block(second, 1)
        acc[blocks[1][2]] += block(second, 2)
        for n in range(2):
            acc[n] += block(first, 3 + n) + block(second, 3 + n)
        for b, terms in enumerate((first, second)):
            for n in range(RANDOM):
                trand[zs * 2 * RANDOM + RANDOM * b + n] = block(terms, 5 + n)

    def wide(ref):
        return ref.astype(jnp.float32)

    def partial_proj():
        with jax.named_scope("attn_back"):
            got(atr.at[pl.ds(0, CHIPS - 1)], AT)
        with jax.named_scope("partial_proj"):
            attn = jnp.concatenate([
                jnp.concatenate([atr[h][:, :HEAD_DIM] for h in range(HEADS)], axis=1),
                jnp.concatenate([atr[h][:, HEAD_DIM:] for h in range(HEADS)], axis=1)], axis=0)
            pp[1] = dot(attn, go_ref[0, :, theirs], ((0,), (0,))).astype(jnp.bfloat16)
            send(pp.at[1], pps, RS, sib)
            pp[0] = dot(attn, go_ref[0, :, mine], ((0,), (0,))).astype(jnp.bfloat16)

    def proj_xy():
        with jax.named_scope("grad_proj_core"):
            got(pps, RS)
            total = wide(pp[0]) + wide(pps[...])
            s1[...] = total.astype(jnp.bfloat16).reshape(ny * nx, 16, HALF)
            rx[dp] = s1[dp]
            for dx in sorted(range(nx), key=lambda d: -min(d, nx - d)):
                for dy in sorted(range(ny), key=lambda d: -min(d, ny - d)):
                    if dx or dy:
                        target = ((y + dy) % ny) * nx + (x + dx) % nx
                        send(s1.at[target], rx.at[dp], RX, (target, s))

    def proj_z():
        with jax.named_scope("grad_proj_xy"):
            got(rx.at[pl.ds(0, ny * nx - 1)], RX)
            total = wide(rx[0])
            for d in range(1, ny * nx):
                total += wide(rx[d])
            s3[...] = total.astype(jnp.bfloat16)
            rz[s] = s3[...]
            for off in FAR:
                send(s3, rz.at[s], RZ, zdev(ahead(off)))
                send(s3, rz.at[s], RZ, (dp, 2 * ahead(off) + other))
            send(s3, rz.at[s], RZ, sib)

    def proj_end():
        with jax.named_scope("grad_proj_z"):
            got(rz.at[pl.ds(0, 2 * CHIPS - 1)], RZ)
            for half in range(2):
                total = wide(rz[half])
                for k in range(1, CHIPS):
                    total += wide(rz[2 * k + half])
                gp_ref[:, half * HALF:(half + 1) * HALF] = total

    with jax.named_scope("queries_wait"):
        got(qr.at[pl.ds(0, CHIPS - 1)], QS)
    with jax.named_scope("attention"):
        for n in range(CHIPS + 2 * PART):
            if n < CHIPS:
                scored(n)
            if PART <= n < CHIPS + PART:
                softmax(n - PART)
            if 2 * PART <= n:
                attended(n - 2 * PART)
        atr[z] = ats[z]
        for off in FAR:
            send(ats.at[ahead(off)], atr.at[z], AT, zdev(ahead(off)))

    with jax.named_scope("grad_attn_wait"):
        got(gr.at[pl.ds(0, CHIPS - 1)], GS)
    with jax.named_scope("score_grads"):
        for zs in range(CHIPS):
            score_grads(zs)
    with jax.named_scope("query_grads"):
        for zs in range(CHIPS):
            query_grads(zs)
        dqr[z] = dqs[z]
        for off in FAR:
            send(dqs.at[ahead(off)], dqr.at[z], DQ, zdev(ahead(off)))
    with jax.named_scope("block_terms"):
        @pl.loop(0, CHIPS // PART)
        def _(step):
            results = [block_terms(step * PART + n) for n in range(PART)]
            for n in range(PART):
                collect(step * PART + n, *results[n])
            pl.when(step == 0)(partial_proj)

    def pull(o):
        parts = [acc[2 * o], acc[2 * o + 1]]
        for zs in range(CHIPS):
            term = trand[zs * 2 * RANDOM + tbls[zs, 0, o]]
            for w in range(2):
                parts[w] += term * tbls[zs, 0, 16 + 16 * w + o].astype(jnp.float32)
        return parts

    with jax.named_scope("other_core_terms"):
        @pl.loop(0, CHIPS)
        def _(step):
            off = (step + 4) % CHIPS
            k = ahead(off)
            parts = pull(2 * k + other)
            for w in range(2):
                xs[k, w] = parts[w].astype(jnp.bfloat16)
            send(xs.at[k], xr.at[k], XK, sib, XKR + off)

    proj_xy()

    with jax.named_scope("own_terms"):
        @pl.loop(0, CHIPS)
        def _(step):
            off = (step + 4) % CHIPS
            k = ahead(off)
            parts = pull(2 * k + c)
            got(xr.at[k], XKR + off)
            for w in range(2):
                dks[k, w] = (parts[w] + xr[k, w].astype(jnp.float32)).astype(jnp.bfloat16)

            @pl.when(off > 0)
            def _():
                send(dks.at[k], dkr.at[z], DK, zdev(k))

        dkr[z] = dks[z]

    proj_z()

    with jax.named_scope("grad_queries"):
        got(dqr.at[pl.ds(0, CHIPS - 1)], DQ)
        gq_ref[0, :BLOCK] = jnp.concatenate([dqr[h][:, :HEAD_DIM] for h in range(HEADS)], axis=1)
        gq_ref[0, BLOCK:] = jnp.concatenate([dqr[h][:, HEAD_DIM:] for h in range(HEADS)], axis=1)

    with jax.named_scope("grad_keys_values"):
        got(dkr.at[pl.ds(0, CHIPS - 1)], DK)
        pieces = [dkr[h].reshape(TOKENS, 128) for h in range(HEADS)]
        gk_ref[0] = jnp.concatenate([p[:, :HEAD_DIM] for p in pieces], axis=1)
        gv_ref[0] = jnp.concatenate([p[:, HEAD_DIM:] for p in pieces], axis=1)

    proj_end()

    with jax.named_scope("sent"):
        rest = pl.ds(0, CHIPS - 1)
        sent(pj.at[0, pl.ds(0, ny - 1), 0], PY)
        sent(pj.at[0, :, pl.ds(0, nx - 1)], PX)
        sent(pj.at[0], PS)
        sent(tblv.at[rest], TBL)
        sent(kvp.at[rest], KVS)
        sent(kvp, KVF)
        sent(qp.at[rest], QS)
        sent(gpk.at[rest], GS)
        sent(ats.at[rest], AT)
        sent(dqs.at[rest], DQ)
        sent(xs, XK)
        sent(dks.at[rest], DK)
        sent(pps, RS)
        sent(rx.at[pl.ds(0, ny * nx - 1)], RX)
        sent(rz.at[pl.ds(0, 2 * CHIPS - 1)], RZ)


def store(*refs):
    count = len(refs) // 2
    copies = [pltpu.make_async_copy(refs[n], refs[count + n], refs[-1].at[n]) for n in range(count)]
    for copy in copies:
        copy.start()
    for copy in copies:
        copy.wait()


def attention_grads(nx, ny, q, k, v, go, rb, proj):
    bf, f32 = jnp.bfloat16, jnp.float32
    rows = nx * ny * 16
    hbm = pl.BlockSpec(memory_space=pltpu.HBM)
    vmem = pl.BlockSpec(memory_space=pltpu.VMEM)
    scratch = [
        pltpu.VMEM((1, TOKENS, WIDTH), bf),
        pltpu.VMEM((1, TOKENS, WIDTH), bf),
        pltpu.VMEM((1, TOKENS, WIDTH), bf),
        pltpu.VMEM((1, TOKENS, WIDTH), bf),
        pltpu.SMEM((1, 2, RANDOM), jnp.int32),
        pltpu.VMEM((16, WIDTH), bf),
        pltpu.VMEM((8, 128), jnp.int32),
        pltpu.VMEM((CHIPS, 8, 128), jnp.int32),
        pltpu.SMEM((CHIPS, 8, 128), jnp.int32),
        pltpu.VMEM((HEADS, 2, BLOCK, 128), bf),
        pltpu.VMEM((BLOCKS, BLOCK, 128), bf),
        pltpu.VMEM((BLOCKS, BLOCK, 128), bf),
        pltpu.VMEM((BLOCKS, BLOCK, 128), bf),
        pltpu.VMEM((HEADS, BLOCK, 128), bf),
        pltpu.VMEM((CHIPS, BLOCK, 128), bf),
        pltpu.VMEM((HEADS, BLOCK, 128), bf),
        pltpu.VMEM((CHIPS, BLOCK, 128), bf),
        pltpu.VMEM((2, ny, nx, 16, HALF), bf),
        pltpu.VMEM((CHIPS, 8 * BLOCK, 128), f32),
        pltpu.VMEM((CHIPS, 8 * BLOCK, 128), bf),
        pltpu.VMEM((CHIPS, 8 * BLOCK, 128), bf),
        pltpu.VMEM((BLOCKS, BLOCK, 128), f32),
        pltpu.VMEM((CHIPS * 2 * RANDOM, BLOCK, 128), f32),
        pltpu.VMEM((CHIPS, BLOCK, 128), bf),
        pltpu.VMEM((HEADS, BLOCK, 128), bf),
        pltpu.VMEM((CHIPS, BLOCK, 128), bf),
        pltpu.VMEM((HEADS, BLOCK, 128), bf),
        pltpu.VMEM((CHIPS, 2, BLOCK, 128), bf),
        pltpu.VMEM((CHIPS, 2, BLOCK, 128), bf),
        pltpu.VMEM((CHIPS, 2, BLOCK, 128), bf),
        pltpu.VMEM((HEADS, 2, BLOCK, 128), bf),
        pltpu.VMEM((2, rows, HALF), bf),
        pltpu.VMEM((rows, HALF), bf),
        pltpu.VMEM((ny * nx, 16, HALF), bf),
        pltpu.VMEM((ny * nx, 16, HALF), bf),
        pltpu.VMEM((16, HALF), bf),
        pltpu.VMEM((2 * CHIPS, 16, HALF), bf),
        pltpu.SemaphoreType.DMA((SENDS,)),
        pltpu.SemaphoreType.DMA((RECVS,)),
        pltpu.SemaphoreType.DMA((7,)),
    ]
    tokens = jax.ShapeDtypeStruct((1, TOKENS, WIDTH), bf)
    shapes = [tokens, tokens, tokens, jax.ShapeDtypeStruct((16, WIDTH), f32)]
    grads = pl.pallas_call(
        functools.partial(kernel, nx, ny),
        out_shape=shapes,
        in_specs=[hbm] * 6,
        out_specs=[vmem, vmem, vmem, vmem],
        scratch_shapes=scratch,
        compiler_params=pltpu.CompilerParams(
            collective_id=0, has_side_effects=True, vmem_limit_bytes=VMEM),
        cost_estimate=pl.CostEstimate(
            flops=2 * 500_000_000, bytes_accessed=2_000_000, transcendentals=600_000),
    )(*[pltpu.with_memory_space_constraint(a, pltpu.HBM) for a in (q, k, v, go, rb, proj)])
    return pl.pallas_call(
        store,
        out_shape=shapes,
        in_specs=[vmem] * 4,
        out_specs=[hbm] * 4,
        scratch_shapes=[pltpu.SemaphoreType.DMA((4,))],
        compiler_params=pltpu.CompilerParams(vmem_limit_bytes=1024 * 1024),
    )(*grads)


def solution(mesh, nx=4, ny=8):
    tokens = P("dp", "seq", None)
    return jax.shard_map(
        functools.partial(attention_grads, nx, ny),
        mesh=mesh,
        in_specs=(tokens, tokens, tokens, tokens, tokens, P("dp", None)),
        out_specs=(tokens, tokens, tokens, P("dp", None)),
        check_vma=False,
    )
```

```python
import functools

import jax
import jax.numpy as jnp
from jax import lax
from jax.experimental import pallas as pl
from jax.experimental.pallas import tpu as pltpu
from jax.sharding import PartitionSpec as P

HEADS = 8
HEAD_DIM = 64
BLOCK = 64
RANDOM = 3
CHIPS = 8
TOKENS = 128
WIDTH = 512
HALF = 256
BLOCKS = 32
SCALE = HEAD_DIM ** (-0.5)
NEG = -1e30
FAR = (4, 3, 5, 2, 6, 1, 7)
PART = 4
VMEM = 40 * 1024 * 1024

KVF, QS, GS, TBL, PY, PX, PS, AT, DQ, XK, DK, RS, RX, RZ, KVS = range(15)
SENDS = 15
KV, XKR, RECVS = 16, 24, 32
EXP2 = SCALE * 1.4426950408889634


def dot(a, b, dims):
    return lax.dot_general(a, b, (dims, ((), ())), preferred_element_type=jnp.float32)


def halves(a, b):
    return jnp.concatenate([a, b], axis=1)


def kernel(nx, ny, q_hbm, k_hbm, v_hbm, go_hbm, rb_hbm, pj_hbm, gq_ref, gk_ref, gv_ref, gp_ref,
           q_ref, k_ref, v_ref, go_ref, rb_ref, pj_ref,
           tblme, tblv, tbls, kvp, kv, kk, vv, qp, qr, gpk, gr, pj, sst, pst, dst, acc, trand, ats, atr, dqs, dqr,
           xs, xr, dks, dkr, pp, pps, s1, rx, s3, rz, ssem, rsem, lsem):
    dp = lax.axis_index("dp")
    s = lax.axis_index("seq")
    z, c = s // 2, s % 2
    y, x = dp // nx, dp % nx
    other = 1 - c
    sib = (dp, 2 * z + other)

    def zdev(zt):
        return (dp, 2 * zt + c)

    def xdev(d):
        return (y * nx + (x + d) % nx, s)

    def ydev(d):
        return (((y + d) % ny) * nx + x, s)

    def send(src, dst, sem, dev, arrival=None):
        arrival = sem if arrival is None else arrival
        copy = pltpu.make_async_remote_copy(
            src_ref=src, dst_ref=dst, send_sem=ssem.at[sem], recv_sem=rsem.at[arrival],
            device_id=dev, device_id_type=pl.DeviceIdType.MESH)
        copy.start()

    def got(dst, sem):
        pltpu.make_async_remote_copy(
            src_ref=dst, dst_ref=dst, send_sem=ssem.at[0], recv_sem=rsem.at[sem],
            device_id=sib, device_id_type=pl.DeviceIdType.MESH).wait_recv()

    def sent(src, sem):
        pltpu.make_async_remote_copy(
            src_ref=src, dst_ref=src, send_sem=ssem.at[sem], recv_sem=rsem.at[0],
            device_id=sib, device_id_type=pl.DeviceIdType.MESH).wait_send()

    def ahead(off):
        return (z + off) % CHIPS

    def behind(off):
        return (z + CHIPS - off) % CHIPS

    barrier = pltpu.get_barrier_semaphore()
    hops = [(min(off, CHIPS - off), zdev(ahead(off))) for off in range(1, CHIPS)]
    hops += [(min(d, ny - d), ydev(d)) for d in range(1, ny)]
    hops += [(min(d, nx - d), xdev(d)) for d in range(1, nx)] + [(0, sib)]
    partners = [dev for _, dev in sorted(hops, key=lambda item: -item[0])]
    for dev in partners:
        pl.semaphore_signal(barrier, inc=1, device_id=dev, device_id_type=pl.DeviceIdType.MESH)

    loads = [pltpu.make_async_copy(a, b, lsem.at[1 + n]) for n, (a, b) in enumerate((
        (pj_hbm, pj_ref), (rb_hbm, rb_ref), (k_hbm, k_ref), (v_hbm, v_ref), (q_hbm, q_ref),
        (go_hbm, go_ref)))]
    for load in loads:
        load.start()

    mine = pl.ds(pl.multiple_of(c * HALF, HALF), HALF)
    theirs = pl.ds(pl.multiple_of(other * HALF, HALF), HALF)

    low = lax.broadcasted_iota(jnp.int32, (BLOCK, 128), 1) < HEAD_DIM

    def swap(a):
        return halves(a[:, HEAD_DIM:], a[:, :HEAD_DIM])

    def fill(source):
        for n in range(2):
            j = 2 * source + n
            pair = kv[j]
            turned = swap(pair)
            kk[j] = jnp.where(low, pair, turned)
            vv[j] = jnp.where(low, turned, pair)

    with jax.named_scope("pack_inputs"):
        loads[0].wait()
        loads[1].wait()
        pj[c, y, x] = pj_ref[:, mine]
        lane = lax.broadcasted_iota(jnp.int32, (8, 128), 1)
        row = jnp.zeros((8, 128), jnp.int32)
        for e in range(2 * RANDOM):
            block = rb_ref[0, e // RANDOM, e % RANDOM]
            own = block // 2
            row = jnp.where(lane == own, e, row)
            row = jnp.where(lane == own + 16 + 16 * (block % 2), 1, row)
            row = jnp.where(lane == 48 + e, block, row)
        tblme[...] = row
        tblv[z] = row
        loads[2].wait()
        loads[3].wait()
        for h in range(HEADS):
            f = slice(h * HEAD_DIM, (h + 1) * HEAD_DIM)
            kvp[h] = halves(k_ref[0, :, f], v_ref[0, :, f]).reshape(2, BLOCK, 128)
        kv[pl.ds(2 * s, 2)] = kvp[z]
        loads[4].wait()
        for h in range(HEADS):
            f = slice(h * HEAD_DIM, (h + 1) * HEAD_DIM)
            qp[h] = halves(q_ref[0, :BLOCK, f], q_ref[0, BLOCK:, f])
        qr[z] = qp[z]
        fill(s)

    with jax.named_scope("barrier"):
        pl.semaphore_wait(barrier, len(partners))

    with jax.named_scope("first_sends"):
        for d in range(1, ny):
            send(pj_ref.at[:, mine], pj.at[c, y, x], PY, ydev(d))
        for off in FAR:
            send(tblme, tblv.at[z], TBL, zdev(ahead(off)))
        for off in FAR:
            zt = ahead(off)
            send(kvp.at[zt], kv.at[pl.ds(2 * s, 2)], KVS, zdev(zt), KV + off)
        send(kvp.at[z], kv.at[pl.ds(2 * s, 2)], KVF, sib)
        for off in FAR:
            zt = ahead(off)
            send(qp.at[zt], qr.at[z], QS, zdev(zt))

    acc[...] = jnp.zeros_like(acc)

    with jax.named_scope("proj_rows_y"):
        got(pj.at[c, pl.ds(0, ny - 1), 0], PY)
        for d in range(1, nx):
            send(pj.at[c, :, x], pj.at[c, :, x], PX, xdev(d))

    with jax.named_scope("tables"):
        got(tblv.at[pl.ds(0, CHIPS - 1)], TBL)
        table = pltpu.make_async_copy(tblv, tbls, lsem.at[0])
        table.start()
    def forward(off):
        zf = behind(off)
        part = kv.at[pl.ds(4 * zf + 2 * c, 2)]
        got(part, KV + off)
        send(part, part, KVF, sib)
        fill(2 * zf + c)

    with jax.named_scope("forward"):
        for off in FAR:
            forward(off)

    with jax.named_scope("proj_rows_x"):
        got(pj.at[c, :, pl.ds(0, nx - 1)], PX)
        send(pj.at[c], pj.at[c], PS, sib)

    with jax.named_scope("proj_other"):
        got(pj.at[other], PS)
        loads[5].wait()
    with jax.named_scope("grad_attn"):
        rows = nx * ny * 16
        ga = dot(go_ref[0, :, :HALF], pj[0].reshape(rows, HALF), ((1,), (1,)))
        ga += dot(go_ref[0, :, HALF:], pj[1].reshape(rows, HALF), ((1,), (1,)))
        ga = ga.astype(jnp.bfloat16)
        for h in range(HEADS):
            f = slice(h * HEAD_DIM, (h + 1) * HEAD_DIM)
            gpk[h] = halves(ga[:BLOCK, f], ga[BLOCK:, f])
        gr[z] = gpk[z]
        for off in FAR:
            zt = ahead(off)
            send(gpk.at[zt], gr.at[z], GS, zdev(zt))

    with jax.named_scope("other_core_keys"):
        table.wait()
        got(kv.at[pl.ds(0, 2 * CHIPS)], KVF)
        for k in range(CHIPS):
            fill(2 * k + other)

    high = jnp.logical_not(low)
    none = jnp.zeros((BLOCK, 128), jnp.bfloat16)

    def diagonal(a, b):
        return jnp.concatenate([jnp.where(low, a, none), jnp.where(high, b, none)], axis=0)

    def slots(zs, b):
        i = 4 * zs + 2 * c + b
        fixed = (jnp.maximum(i - 1, 0), i, jnp.minimum(i + 1, BLOCKS - 1), 0, 1)
        return i, fixed, [tbls[zs, 0, 48 + RANDOM * b + n] for n in range(RANDOM)]

    def paired(ref, blocks):
        return jnp.concatenate(
            [jnp.where(low, ref[a], ref[b]) for a, b in zip(*blocks)], axis=0)

    def named(zs):
        return [list(fixed) + ids for _, fixed, ids in (slots(zs, b) for b in range(2))]

    def biases(zs):
        both = []
        for b in range(2):
            i, fixed, ids = slots(zs, b)
            valid = [i >= 1, i >= 0, i < BLOCKS - 1, i >= 2, i >= 3]
            for n in range(RANDOM):
                r = ids[n]
                clash = (r == i - 1) | (r == i) | (r == i + 1) | (r <= 1)
                for earlier in ids[:n]:
                    clash = clash | (r == earlier)
                valid.append(jnp.logical_not(clash))
            both.append([jnp.where(v, 0.0, NEG) for v in valid])
        return both

    def block(a, n):
        return a[n * BLOCK:(n + 1) * BLOCK]

    def fold(out):
        return jnp.where(low, block(out, 0), block(out, 1)).astype(jnp.bfloat16)

    def scored(zs):
        bias = biases(zs)
        scores = dot(paired(kk, named(zs)), diagonal(qr[zs], qr[zs]), ((1,), (1,)))
        sst[zs] = jnp.concatenate([
            block(scores, n) + jnp.where(low[:1], bias[0][n], bias[1][n]) for n in range(8)], axis=0)

    def softmax(zs):
        scores = sst[zs]
        top = jnp.max(scores, axis=0, keepdims=True)
        e = jnp.exp2((scores - top) * EXP2)
        pst[zs] = (e * (1.0 / jnp.sum(e, axis=0, keepdims=True))).astype(jnp.bfloat16)

    def attended(zs):
        ats[zs] = fold(dot(pst[zs], paired(vv, named(zs)), ((0,), (0,))))

    def score_grads(zs):
        gf = gr[zs]
        dprob = dot(paired(vv, named(zs)), diagonal(gf, gf) * SCALE, ((1,), (1,)))
        prob = pst[zs].astype(jnp.float32)
        delta = jnp.sum(prob * dprob, axis=0, keepdims=True)
        dst[zs] = (prob * (dprob - delta)).astype(jnp.bfloat16)

    def query_grads(zs):
        dqs[zs] = fold(dot(dst[zs], paired(kk, named(zs)), ((0,), (0,))))

    def block_terms(zs):
        qf, gf = qr[zs], gr[zs]
        prob, dscore = pst[zs], dst[zs]
        left = jnp.concatenate([low] * 8, axis=0)
        first = dot(jnp.where(left, dscore, swap(prob)), diagonal(qf, swap(gf)), ((1,), (0,)))
        second = dot(jnp.where(left, swap(dscore), prob), diagonal(swap(qf), gf), ((1,), (0,)))
        return first, second

    def collect(zs, first, second):
        blocks = named(zs)
        acc[blocks[0][0]] += block(first, 0)
        acc[blocks[0][1]] += block(first, 1) + block(second, 0)
        acc[blocks[1][1]] += block(first, 2) + block(second, 1)
        acc[blocks[1][2]] += block(second, 2)
        for n in range(2):
            acc[n] += block(first, 3 + n) + block(second, 3 + n)
        for b, terms in enumerate((first, second)):
            for n in range(RANDOM):
                trand[zs * 2 * RANDOM + RANDOM * b + n] = block(terms, 5 + n)

    def wide(ref):
        return ref.astype(jnp.float32)

    def partial_proj():
        with jax.named_scope("attn_back"):
            got(atr.at[pl.ds(0, CHIPS - 1)], AT)
        with jax.named_scope("partial_proj"):
            attn = jnp.concatenate([
                jnp.concatenate([atr[h][:, :HEAD_DIM] for h in range(HEADS)], axis=1),
                jnp.concatenate([atr[h][:, HEAD_DIM:] for h in range(HEADS)], axis=1)], axis=0)
            for first in range(0, WIDTH, HALF):
                upper = attn[:, first:first + HALF]
                part = pl.ds(first, HALF)
                pp[1, part] = dot(upper, go_ref[0, :, theirs], ((0,), (0,))).astype(jnp.bfloat16)
                send(pp.at[1, part], pps.at[part], RS, sib)
            pp[0] = dot(attn, go_ref[0, :, mine], ((0,), (0,))).astype(jnp.bfloat16)

    def proj_xy():
        with jax.named_scope("grad_proj_core"):
            got(pps, RS)
            total = wide(pp[0]) + wide(pps[...])
            s1[...] = total.astype(jnp.bfloat16).reshape(ny * nx, 16, HALF)
            rx[dp] = s1[dp]
            for dx in sorted(range(nx), key=lambda d: -min(d, nx - d)):
                for dy in sorted(range(ny), key=lambda d: -min(d, ny - d)):
                    if dx or dy:
                        target = ((y + dy) % ny) * nx + (x + dx) % nx
                        send(s1.at[target], rx.at[dp], RX, (target, s))

    def proj_z():
        with jax.named_scope("grad_proj_xy"):
            got(rx.at[pl.ds(0, ny * nx - 1)], RX)
            total = wide(rx[0])
            for d in range(1, ny * nx):
                total += wide(rx[d])
            s3[...] = total.astype(jnp.bfloat16)
            rz[s] = s3[...]
            for off in FAR:
                send(s3, rz.at[s], RZ, zdev(ahead(off)))
                send(s3, rz.at[s], RZ, (dp, 2 * ahead(off) + other))
            send(s3, rz.at[s], RZ, sib)

    def proj_end():
        with jax.named_scope("grad_proj_z"):
            got(rz.at[pl.ds(0, 2 * CHIPS - 1)], RZ)
            for half in range(2):
                total = wide(rz[half])
                for k in range(1, CHIPS):
                    total += wide(rz[2 * k + half])
                gp_ref[:, half * HALF:(half + 1) * HALF] = total

    with jax.named_scope("queries_wait"):
        got(qr.at[pl.ds(0, CHIPS - 1)], QS)
    with jax.named_scope("attention"):
        for n in range(CHIPS + 2 * PART):
            if n < CHIPS:
                scored(n)
            if PART <= n < CHIPS + PART:
                softmax(n - PART)
            if 2 * PART <= n:
                attended(n - 2 * PART)
        atr[z] = ats[z]
        for off in FAR:
            send(ats.at[ahead(off)], atr.at[z], AT, zdev(ahead(off)))

    with jax.named_scope("grad_attn_wait"):
        got(gr.at[pl.ds(0, CHIPS - 1)], GS)
    with jax.named_scope("score_grads"):
        for zs in range(CHIPS):
            score_grads(zs)
    with jax.named_scope("query_grads"):
        for zs in range(CHIPS):
            query_grads(zs)
        dqr[z] = dqs[z]
        for off in FAR:
            send(dqs.at[ahead(off)], dqr.at[z], DQ, zdev(ahead(off)))
    with jax.named_scope("block_terms"):
        @pl.loop(0, CHIPS // PART)
        def _(step):
            results = [block_terms(step * PART + n) for n in range(PART)]
            for n in range(PART):
                collect(step * PART + n, *results[n])
            pl.when(step == 0)(partial_proj)

    def pull(o):
        parts = [acc[2 * o], acc[2 * o + 1]]
        for zs in range(CHIPS):
            term = trand[zs * 2 * RANDOM + tbls[zs, 0, o]]
            for w in range(2):
                parts[w] += term * tbls[zs, 0, 16 + 16 * w + o].astype(jnp.float32)
        return parts

    with jax.named_scope("other_core_terms"):
        @pl.loop(0, CHIPS)
        def _(step):
            off = (step + 4) % CHIPS
            k = ahead(off)
            parts = pull(2 * k + other)
            for w in range(2):
                xs[k, w] = parts[w].astype(jnp.bfloat16)
            send(xs.at[k], xr.at[k], XK, sib, XKR + off)

    proj_xy()

    with jax.named_scope("own_terms"):
        @pl.loop(0, CHIPS)
        def _(step):
            off = (step + 4) % CHIPS
            k = ahead(off)
            parts = pull(2 * k + c)
            got(xr.at[k], XKR + off)
            for w in range(2):
                dks[k, w] = (parts[w] + xr[k, w].astype(jnp.float32)).astype(jnp.bfloat16)

            @pl.when(off > 0)
            def _():
                send(dks.at[k], dkr.at[z], DK, zdev(k))

        dkr[z] = dks[z]

    proj_z()

    with jax.named_scope("grad_queries"):
        got(dqr.at[pl.ds(0, CHIPS - 1)], DQ)
        gq_ref[0, :BLOCK] = jnp.concatenate([dqr[h][:, :HEAD_DIM] for h in range(HEADS)], axis=1)
        gq_ref[0, BLOCK:] = jnp.concatenate([dqr[h][:, HEAD_DIM:] for h in range(HEADS)], axis=1)

    with jax.named_scope("grad_keys_values"):
        got(dkr.at[pl.ds(0, CHIPS - 1)], DK)
        pieces = [dkr[h].reshape(TOKENS, 128) for h in range(HEADS)]
        gk_ref[0] = jnp.concatenate([p[:, :HEAD_DIM] for p in pieces], axis=1)
        gv_ref[0] = jnp.concatenate([p[:, HEAD_DIM:] for p in pieces], axis=1)

    proj_end()

    with jax.named_scope("sent"):
        rest = pl.ds(0, CHIPS - 1)
        sent(pj.at[0, pl.ds(0, ny - 1), 0], PY)
        sent(pj.at[0, :, pl.ds(0, nx - 1)], PX)
        sent(pj.at[0], PS)
        sent(tblv.at[rest], TBL)
        sent(kvp.at[rest], KVS)
        sent(kvp, KVF)
        sent(qp.at[rest], QS)
        sent(gpk.at[rest], GS)
        sent(ats.at[rest], AT)
        sent(dqs.at[rest], DQ)
        sent(xs, XK)
        sent(dks.at[rest], DK)
        sent(pps, RS)
        sent(rx.at[pl.ds(0, ny * nx - 1)], RX)
        sent(rz.at[pl.ds(0, 2 * CHIPS - 1)], RZ)


def store(*refs):
    count = len(refs) // 2
    copies = [pltpu.make_async_copy(refs[n], refs[count + n], refs[-1].at[n]) for n in range(count)]
    for copy in copies:
        copy.start()
    for copy in copies:
        copy.wait()


def attention_grads(nx, ny, q, k, v, go, rb, proj):
    bf, f32 = jnp.bfloat16, jnp.float32
    rows = nx * ny * 16
    hbm = pl.BlockSpec(memory_space=pltpu.HBM)
    vmem = pl.BlockSpec(memory_space=pltpu.VMEM)
    scratch = [
        pltpu.VMEM((1, TOKENS, WIDTH), bf),
        pltpu.VMEM((1, TOKENS, WIDTH), bf),
        pltpu.VMEM((1, TOKENS, WIDTH), bf),
        pltpu.VMEM((1, TOKENS, WIDTH), bf),
        pltpu.SMEM((1, 2, RANDOM), jnp.int32),
        pltpu.VMEM((16, WIDTH), bf),
        pltpu.VMEM((8, 128), jnp.int32),
        pltpu.VMEM((CHIPS, 8, 128), jnp.int32),
        pltpu.SMEM((CHIPS, 8, 128), jnp.int32),
        pltpu.VMEM((HEADS, 2, BLOCK, 128), bf),
        pltpu.VMEM((BLOCKS, BLOCK, 128), bf),
        pltpu.VMEM((BLOCKS, BLOCK, 128), bf),
        pltpu.VMEM((BLOCKS, BLOCK, 128), bf),
        pltpu.VMEM((HEADS, BLOCK, 128), bf),
        pltpu.VMEM((CHIPS, BLOCK, 128), bf),
        pltpu.VMEM((HEADS, BLOCK, 128), bf),
        pltpu.VMEM((CHIPS, BLOCK, 128), bf),
        pltpu.VMEM((2, ny, nx, 16, HALF), bf),
        pltpu.VMEM((CHIPS, 8 * BLOCK, 128), f32),
        pltpu.VMEM((CHIPS, 8 * BLOCK, 128), bf),
        pltpu.VMEM((CHIPS, 8 * BLOCK, 128), bf),
        pltpu.VMEM((BLOCKS, BLOCK, 128), f32),
        pltpu.VMEM((CHIPS * 2 * RANDOM, BLOCK, 128), f32),
        pltpu.VMEM((CHIPS, BLOCK, 128), bf),
        pltpu.VMEM((HEADS, BLOCK, 128), bf),
        pltpu.VMEM((CHIPS, BLOCK, 128), bf),
        pltpu.VMEM((HEADS, BLOCK, 128), bf),
        pltpu.VMEM((CHIPS, 2, BLOCK, 128), bf),
        pltpu.VMEM((CHIPS, 2, BLOCK, 128), bf),
        pltpu.VMEM((CHIPS, 2, BLOCK, 128), bf),
        pltpu.VMEM((HEADS, 2, BLOCK, 128), bf),
        pltpu.VMEM((2, rows, HALF), bf),
        pltpu.VMEM((rows, HALF), bf),
        pltpu.VMEM((ny * nx, 16, HALF), bf),
        pltpu.VMEM((ny * nx, 16, HALF), bf),
        pltpu.VMEM((16, HALF), bf),
        pltpu.VMEM((2 * CHIPS, 16, HALF), bf),
        pltpu.SemaphoreType.DMA((SENDS,)),
        pltpu.SemaphoreType.DMA((RECVS,)),
        pltpu.SemaphoreType.DMA((7,)),
    ]
    tokens = jax.ShapeDtypeStruct((1, TOKENS, WIDTH), bf)
    shapes = [tokens, tokens, tokens, jax.ShapeDtypeStruct((16, WIDTH), f32)]
    grads = pl.pallas_call(
        functools.partial(kernel, nx, ny),
        out_shape=shapes,
        in_specs=[hbm] * 6,
        out_specs=[vmem, vmem, vmem, vmem],
        scratch_shapes=scratch,
        compiler_params=pltpu.CompilerParams(
            collective_id=0, has_side_effects=True, vmem_limit_bytes=VMEM),
        cost_estimate=pl.CostEstimate(
            flops=2 * 500_000_000, bytes_accessed=2_000_000, transcendentals=600_000),
    )(*[pltpu.with_memory_space_constraint(a, pltpu.HBM) for a in (q, k, v, go, rb, proj)])
    return pl.pallas_call(
        store,
        out_shape=shapes,
        in_specs=[vmem] * 4,
        out_specs=[hbm] * 4,
        scratch_shapes=[pltpu.SemaphoreType.DMA((4,))],
        compiler_params=pltpu.CompilerParams(vmem_limit_bytes=1024 * 1024),
    )(*grads)


def solution(mesh, nx=4, ny=8):
    tokens = P("dp", "seq", None)
    return jax.shard_map(
        functools.partial(attention_grads, nx, ny),
        mesh=mesh,
        in_specs=(tokens, tokens, tokens, tokens, tokens, P("dp", None)),
        out_specs=(tokens, tokens, tokens, P("dp", None)),
        check_vma=False,
    )
```
